512 devices in a mesh: row: 16 (over x, z_hi, core), col: 32 (over z_lo, y).
Axes of the slice: x: 4, y: 4, z: 16 (z_hi: 2, z_lo: 8; z = z_hi * 8 + z_lo), core: 2. Of those that a mesh axis runs over, the one named last changes fastest.
Arguments:
- pair_state: bfloat16 [384, 384, 128], P('row', 'col'), may hold values from -6 to 6
- outgoing_input: bfloat16 [128, 640], replicated, may hold values from -0.5 to 0.5
- outgoing_output: bfloat16 [128, 128], replicated, may hold values from -0.5 to 0.5
- incoming_input: bfloat16 [128, 640], replicated, may hold values from -0.5 to 0.5
- incoming_output: bfloat16 [128, 128], replicated, may hold values from -0.5 to 0.5
- transition_input: bfloat16 [128, 1024], replicated, may hold values from -0.5 to 0.5
- transition_output: bfloat16 [512, 128], replicated, may hold values from -0.25 to 0.25
Outputs:
- pair_result: bfloat16 [384, 384, 128], P('row', 'col')
The draws below stay inside these ranges and needn't reach their ends.
All inputs are finite; a program needn't handle non-finite values.
Results may differ from the reference program's by a relative error of at most 0.02.
Values may be sent and summed in bfloat16 or wider, within the bound.
A program may use at most 64 MiB of HBM per device.

```python
from functools import partial
import jax
import jax.numpy as jnp
from jax import lax

C = 128
TRANS = 512
N = 384


def block_scale(key, shape, pieces, low, largest):
    factor_of, own = 1.0, jax.random.fold_in(key, 6)
    for dim, parts in pieces:
        draws = jnp.exp(jax.random.uniform(jax.random.fold_in(own, dim), (parts,), jnp.float32, low / len(pieces), largest / len(pieces)))
        factor_of = factor_of * jnp.repeat(draws, shape[dim] // parts).reshape([-1 if axis == dim else 1 for axis in range(len(shape))])
    return factor_of


def scatter_about(stream_key, extent, width, bound, split=(), held_as=jnp.bfloat16):
    array = width * jax.random.normal(stream_key, extent, jnp.float32)
    if split:
        array = array * block_scale(stream_key, extent, split, -0.22, 0.18)
    return jnp.clip(array, -bound, bound).astype(held_as)


def setup_inputs(seed: int = 0) -> dict:
    seeds = jax.random.split(jax.random.key(seed), 8)
    pair_state = scatter_about(seeds[0], (N, N, C), 1.0, 6.0, ((0, 16), (1, 32)))
    outgoing_input = scatter_about(seeds[1], (C, 5 * C), C ** -0.5, 0.5)
    outgoing_output = scatter_about(seeds[2], (C, C), C ** -0.5, 0.5)
    incoming_input = scatter_about(seeds[3], (C, 5 * C), C ** -0.5, 0.5)
    incoming_output = scatter_about(seeds[4], (C, C), C ** -0.5, 0.5)
    transition_input = scatter_about(seeds[5], (C, 2 * TRANS), C ** -0.5, 0.5)
    transition_output = scatter_about(seeds[6], (TRANS, C), TRANS ** -0.5, 0.25)
    return {"pair_state": pair_state, "outgoing_input": outgoing_input, "outgoing_output": outgoing_output, "incoming_input": incoming_input, "incoming_output": incoming_output, "transition_input": transition_input, "transition_output": transition_output}


norm_eps = 1e-05

def layer_norm(values):
    centred = values - lax.optimization_barrier(jnp.mean(values, axis=-1, keepdims=True))
    spread = lax.optimization_barrier(jnp.mean(centred * centred, axis=-1, keepdims=True))
    return centred * lax.rsqrt(spread + norm_eps)

def project_rows(state_row, weight):
    channels = state_row.shape[-1]
    normed = layer_norm(state_row.astype(jnp.float32)).astype(jnp.bfloat16)
    projected = jnp.dot(normed, weight, preferred_element_type=jnp.float32)
    left_edge = (jax.nn.sigmoid(projected[:, :channels]) * projected[:, channels:2 * channels]).astype(jnp.bfloat16)
    right_edge = (jax.nn.sigmoid(projected[:, 2 * channels:3 * channels]) * projected[:, 3 * channels:4 * channels]).astype(jnp.bfloat16)
    out_gate = jax.nn.sigmoid(projected[:, 4 * channels:])
    return (left_edge, right_edge, out_gate)

def finish_rows(inputs, weight):
    state_row, combined_row, gate_row = inputs
    normed = layer_norm(combined_row).astype(jnp.bfloat16)
    update = jnp.dot(normed, weight, preferred_element_type=jnp.float32)
    return (state_row.astype(jnp.float32) + gate_row * update).astype(jnp.bfloat16)

def triangle(state, weight_in, weight_out, outgoing):
    left_edge, right_edge, out_gate = lax.map(partial(project_rows, weight=weight_in), state)
    left_wide = left_edge.astype(jnp.float32)
    right_wide = right_edge.astype(jnp.float32)
    if outgoing:
        combined = jnp.einsum('ikc,jkc->ijc', left_wide, right_wide)
    else:
        combined = jnp.einsum('kic,kjc->ijc', left_wide, right_wide)
    return lax.map(partial(finish_rows, weight=weight_out), (state, combined, out_gate))

def transition_rows(state_row, weight_in, weight_out):
    hidden_units = weight_out.shape[0]
    normed = layer_norm(state_row.astype(jnp.float32)).astype(jnp.bfloat16)
    hidden = jnp.dot(normed, weight_in, preferred_element_type=jnp.float32)
    mixed = (jax.nn.silu(hidden[:, :hidden_units]) * hidden[:, hidden_units:]).astype(jnp.bfloat16)
    return (state_row.astype(jnp.float32) + jnp.dot(mixed, weight_out, preferred_element_type=jnp.float32)).astype(jnp.bfloat16)

def reference(pair_state, outgoing_input, outgoing_output, incoming_input, incoming_output, transition_input, transition_output):
    after_out = triangle(pair_state, outgoing_input, outgoing_output, True)
    after_in = triangle(after_out, incoming_input, incoming_output, False)
    return lax.map(partial(transition_rows, weight_in=transition_input, weight_out=transition_output), after_in)
```

```python
import jax
import jax.numpy as jnp
from jax import lax
from jax.experimental import pallas as pl
from jax.experimental.pallas import tpu as pltpu
from jax.sharding import PartitionSpec as P

MESH = pl.DeviceIdType.MESH
norm_eps = 1e-05
f32 = jnp.float32
bf16 = jnp.bfloat16


def roll_lanes(values, shift):
    return pltpu.roll(values, shift, 1)


def swap_lanes(parts, width, roll):
    lane = lax.broadcasted_iota(jnp.int32, parts[0].shape, 1)
    parts = list(parts)
    for bit in (1, 2, 4):
        low = (lane & (bit * width)) == 0
        for a in range(8):
            if a & bit == 0:
                first, second = parts[a], parts[a | bit]
                parts[a] = jnp.where(low, first, roll(second, bit * width))
                parts[a | bit] = jnp.where(low, roll(first, 128 - bit * width), second)
    return parts


def layer_norm(values):
    centred = values - jnp.mean(values, axis=-1, keepdims=True)
    spread = jnp.mean(centred * centred, axis=-1, keepdims=True)
    return centred * lax.rsqrt(spread + norm_eps)


def nt(a, b):
    return lax.dot_general(a, b, (((1,), (1,)), ((), ())), preferred_element_type=f32)


def nn(a, b):
    return jnp.dot(a, b, preferred_element_type=f32)


def widen(rows, columns):
    row = lax.broadcasted_iota(jnp.int32, (rows, columns), 0)
    column = lax.broadcasted_iota(jnp.int32, (rows, columns), 1)
    inside = column & 15
    hit = (row == (column >> 4) * 12 + inside) & (inside < 12)
    return jnp.where(hit, 1.0, 0.0).astype(bf16)


def channel_order():
    row = lax.broadcasted_iota(jnp.int32, (128, 128), 0)
    column = lax.broadcasted_iota(jnp.int32, (128, 128), 1)
    return jnp.where(column == (row & 7) * 16 + (row >> 3), 1.0, 0.0).astype(bf16)


def edges(normed, w_t):
    ordered = jnp.concatenate(
        [normed[(il * 3 + ih) * 16 : (il * 3 + ih + 1) * 16] for ih in range(3) for il in range(8)], axis=0
    )
    projected = nt(w_t, ordered)
    left = jax.nn.sigmoid(projected[0:128]) * projected[128:256]
    right = jax.nn.sigmoid(projected[256:384]) * projected[384:512]
    return left.astype(bf16), right.astype(bf16)


def regroup(blocks, roll):
    for core in range(2):
        for ih in range(3):
            parts = swap_lanes([blocks(core, s, y, ih) for s in range(2) for y in range(4)], 16, roll)
            for il in range(8):
                yield core * 24 + ih * 8 + il, parts[il]


def split_pair(first, second, roll):
    low = lax.broadcasted_iota(jnp.int32, first.shape, 1) < 64
    return jnp.where(low, first, roll(second, 64)), jnp.where(low, roll(first, 64), second)


def product_out(left, right):
    total = nt(left, right).astype(bf16)
    return nn(total, widen(384, 512))


def product_in(left, right):
    turned = nt(widen(96, 128), left).astype(bf16)
    return nn(turned, right)


def parcels(total, roll):
    for zh in range(2):
        for t in range(4):
            tile = total[zh * 48 : (zh + 1) * 48, t * 128 : (t + 1) * 128]
            even, odd = split_pair(tile[0:24], tile[24:48], roll)
            yield zh * 8 + 2 * t, even
            yield zh * 8 + 2 * t + 1, odd


def finish(state, combined, gate, weight):
    update = nn(layer_norm(combined).astype(bf16), weight)
    return (state.astype(f32) + gate * update).astype(bf16)


def kernel(
    x_ref, w1_ref, o1_ref, w2_ref, o2_ref, t1_ref, t2_ref, out_ref,
    a1s, a1r, a2f, a2s, a2r, l2, l2s, bl, br, c1s, c1r, c2s, c2r,
    a1_send, a1_recv, a2_send, a2_recv, b_send, b_recv, bl_send, bl_recv, c1_send, c1_recv, c2_send, c2_recv,
):
    row, col = lax.axis_index("row"), lax.axis_index("col")
    x, zh, core = row // 4, (row // 2) % 2, row % 2
    zl, y = col // 4, col % 4
    z, p = zh * 8 + zl, y * 2 + core

    def at_p(other):
        return ((x * 2 + zh) * 2 + other % 2, zl * 4 + other // 2)

    def at_z(other):
        return ((x * 2 + other // 8) * 2 + core, (other % 8) * 4 + y)

    def at_x(other):
        return ((other * 2 + zh) * 2 + core, col)

    barrier = pltpu.get_barrier_semaphore()
    for me, count, place in ((p, 8, at_p), (z, 16, at_z), (x, 4, at_x)):
        for step in range(1, count):
            pl.semaphore_signal(
                barrier, inc=1, device_id=place(lax.rem(me + step, count)), device_id_type=MESH
            )

    sent = []

    def exchange(source, target, me, count, place, send, recv):
        for step in range(1, count):
            other = lax.rem(me + step, count)
            copy = pltpu.make_async_remote_copy(
                src_ref=source(other), dst_ref=target.at[me], send_sem=send.at[step], recv_sem=recv.at[me],
                device_id=place(other), device_id_type=MESH,
            )
            copy.start()
            sent.append(copy)

    def arrive(source, target, me, count, place, send, recv):
        for step in range(1, count):
            other = lax.rem(me + step, count)
            pltpu.make_async_remote_copy(
                src_ref=source(other), dst_ref=target.at[other], send_sem=send.at[step], recv_sem=recv.at[other],
                device_id=place(other), device_id_type=MESH,
            ).wait_recv()

    def triangle(n, state, w_ref, o_ref):
        normed = layer_norm(state.astype(f32)).astype(bf16)
        left, right = edges(normed, w_ref[:, 0:512].T)
        for other in range(8):
            for s, edge in enumerate((left, right)):
                for ih in range(3):
                    a1s[n, other, s, ih] = edge[other * 16 : other * 16 + 16, ih * 128 : ih * 128 + 128]
        if n == 0:
            pl.semaphore_wait(barrier, 25)
        a1 = (lambda other: a1s.at[n, other], a1r.at[n], p, 8, at_p, a1_send.at[n], a1_recv.at[n])
        exchange(*a1)
        a1r[n, p] = a1s[n, p]
        gate = jax.nn.sigmoid(nn(normed, w_ref[:, 512:640]))
        weight = nn(channel_order(), o_ref[...]).astype(bf16)
        arrive(*a1)

        for i, rows in regroup(lambda core, s, y, ih: a1r[n, y * 2 + core, s, ih].astype(f32), roll_lanes):
            a2f[pl.ds(i, 16, stride=48), :] = rows
        for c in range(16):
            a2s[n, c] = a2f[c * 48 : c * 48 + 48, :].astype(bf16)
        a2 = (lambda other: a2s.at[n, other], a2r.at[n], z, 16, at_z, a2_send.at[n], a2_recv.at[n])
        exchange(*a2)
        a2r[n, z] = a2s[n, z]
        arrive(*a2)

        for half in range(2):
            for t in range(4):
                first, second = split_pair(
                    a2r[n, half * 8 + 2 * t].astype(f32), a2r[n, half * 8 + 2 * t + 1].astype(f32), roll_lanes
                )
                l2s[n, t, half * 48 : half * 48 + 48, :] = first.astype(bf16)
                l2[n, half * 48 : half * 48 + 48, t * 128 : t * 128 + 128] = second.astype(bf16)
        b = (lambda other: l2.at[n], br.at[n], x, 4, at_x, b_send.at[n], b_recv.at[n])
        exchange(*b)
        if n == 1:
            bl_args = (lambda other: l2s.at[n, other], bl, x, 4, at_x, bl_send, bl_recv)
            exchange(*bl_args)
            bl[x] = l2s[n, x]
        br[n, x] = l2[n]
        arrive(*b)
        rights = jnp.concatenate([br[n, other] for other in range(4)], axis=0)
        if n == 0:
            lefts = jnp.concatenate([l2s[n, t] for t in range(4)], axis=1)
            total = product_out(lefts, rights)
        else:
            arrive(*bl_args)
            total = product_in(jnp.concatenate([bl[other] for other in range(4)], axis=0), rights)

        for other, rows in parcels(total, roll_lanes):
            c1s[n, other] = rows.astype(bf16)
        c1 = (lambda other: c1s.at[n, other], c1r.at[n], z, 16, at_z, c1_send.at[n], c1_recv.at[n])
        exchange(*c1)
        c1r[n, z] = c1s[n, z]
        arrive(*c1)
        received = [c1r[n, c].astype(f32) for c in range(16)]
        for ih in range(3):
            turned = jnp.concatenate([part[ih * 8 : ih * 8 + 8] for part in received], axis=0).T
            for there in range(2):
                for far in range(4):
                    start = (there * 4 + far) * 16
                    c2s[n, far * 2 + there, ih] = turned[start : start + 16].astype(bf16)
        c2 = (lambda other: c2s.at[n, other], c2r.at[n], p, 8, at_p, c2_send.at[n], c2_recv.at[n])
        exchange(*c2)
        c2r[n, p] = c2s[n, p]
        arrive(*c2)
        parts = swap_lanes([c2r[n, s].reshape(48, 128).astype(f32) for s in range(8)], 1, roll_lanes)
        return finish(state, jnp.concatenate(parts, axis=0), gate, weight)

    state = x_ref[...].reshape(384, 128)
    state = triangle(0, state, w1_ref, o1_ref)
    state = triangle(1, state, w2_ref, o2_ref)
    normed = layer_norm(state.astype(f32)).astype(bf16)
    hidden = nn(normed, t1_ref[...])
    mixed = (jax.nn.silu(hidden[:, :512]) * hidden[:, 512:]).astype(bf16)
    result = (state.astype(f32) + nn(mixed, t2_ref[...])).astype(bf16)
    out_ref[...] = result.reshape(8, 3, 16, 128)
    for copy in sent:
        copy.wait_send()


def body(pair_state, *weights):
    x = jnp.pad(pair_state, ((0, 0), (0, 4), (0, 0))).reshape(3, 8, 16, 128).transpose(1, 0, 2, 3)
    dma = pltpu.SemaphoreType.DMA
    out = pl.pallas_call(
        kernel,
        out_shape=jax.ShapeDtypeStruct((8, 3, 16, 128), bf16),
        in_specs=[pl.BlockSpec(memory_space=pltpu.VMEM)] * 7,
        out_specs=pl.BlockSpec(memory_space=pltpu.VMEM),
        scratch_shapes=[
            pltpu.VMEM((2, 8, 2, 3, 16, 128), bf16),
            pltpu.VMEM((2, 8, 2, 3, 16, 128), bf16),
            pltpu.VMEM((768, 128), f32),
            pltpu.VMEM((2, 16, 48, 128), bf16),
            pltpu.VMEM((2, 16, 48, 128), bf16),
            pltpu.VMEM((2, 96, 512), bf16),
            pltpu.VMEM((2, 4, 96, 128), bf16),
            pltpu.VMEM((4, 96, 128), bf16),
            pltpu.VMEM((2, 4, 96, 512), bf16),
            pltpu.VMEM((2, 16, 24, 128), bf16),
            pltpu.VMEM((2, 16, 24, 128), bf16),
            pltpu.VMEM((2, 8, 3, 16, 128), bf16),
            pltpu.VMEM((2, 8, 3, 16, 128), bf16),
            dma((2, 8)), dma((2, 8)),
            dma((2, 16)), dma((2, 16)),
            dma((2, 4)), dma((2, 4)),
            dma((4,)), dma((4,)),
            dma((2, 16)), dma((2, 16)),
            dma((2, 8)), dma((2, 8)),
        ],
        compiler_params=pltpu.CompilerParams(
            collective_id=0, has_side_effects=True, vmem_limit_bytes=48 * 2**20
        ),
    )(x, *weights)
    return out.transpose(1, 0, 2, 3).reshape(24, 16, 128)[:, :12]


def solution(mesh):
    placed = (P("row", "col", None), P(), P(), P(), P(), P(), P())
    return jax.shard_map(
        body, mesh=mesh, in_specs=placed, out_specs=P("row", "col", None), check_vma=False
    )
```

```python
import jax
import jax.numpy as jnp
from jax import lax
from jax.experimental import pallas as pl
from jax.experimental.pallas import tpu as pltpu
from jax.sharding import PartitionSpec as P

MESH = pl.DeviceIdType.MESH
norm_eps = 1e-05
f32 = jnp.float32
bf16 = jnp.bfloat16

Z_STEPS = (8, 7, 9, 6, 10, 5, 11, 4, 12, 3, 13, 2, 14, 1, 15)
RING = (2, 1, 3, 0)
P_STEPS = tuple((0, dy, dc) for dy in RING for dc in (1, 0) if (dy, dc) != (0, 0))
G_STEPS = tuple(
    sorted(
        ((dx, dy, dc) for dx in RING for dy in RING for dc in (1, 0) if (dx, dy, dc) != (0, 0, 0)),
        key=lambda step: -(min(step[0], 4 - step[0]) + min(step[1], 4 - step[1])),
    )
)


def roll_lanes(values, shift):
    return pltpu.roll(values, shift, 1)


def swap_lanes(parts, width, roll, bits=(1, 2, 4)):
    lane = lax.broadcasted_iota(jnp.int32, parts[0].shape, 1)
    parts = list(parts)
    for bit in bits:
        low = (lane & (bit * width)) == 0
        for a in range(len(parts)):
            if a & bit == 0:
                first, second = parts[a], parts[a | bit]
                parts[a] = jnp.where(low, first, roll(second, bit * width))
                parts[a | bit] = jnp.where(low, roll(first, 128 - bit * width), second)
    return parts


def layer_norm(values):
    centred = values - jnp.mean(values, axis=-1, keepdims=True)
    spread = jnp.mean(centred * centred, axis=-1, keepdims=True)
    return centred * lax.rsqrt(spread + norm_eps)


def nt(a, b):
    return lax.dot_general(a, b, (((1,), (1,)), ((), ())), preferred_element_type=f32)


def nn(a, b):
    return jnp.dot(a, b, preferred_element_type=f32)


def ones_where(shape, row_of):
    row = lax.broadcasted_iota(jnp.int32, shape, 0)
    column = lax.broadcasted_iota(jnp.int32, shape, 1)
    return jnp.where((row == row_of(column)) & ((column & 15) < 12), 1.0, 0.0).astype(bf16)


def column_places():
    return ones_where(
        (384, 512),
        lambda n: ((n >> 5) & 3) * 96 + (n >> 8) * 48 + ((n >> 4) & 1) * 24 + ((n >> 7) & 1) * 12 + (n & 15),
    )


def row_places():
    return ones_where((96, 128), lambda n: (n >> 6) * 48 + ((n >> 4) & 1) * 24 + ((n >> 5) & 1) * 12 + (n & 15))


def tight():
    return ones_where((384, 512), lambda n: (n >> 4) * 12 + (n & 15))


def order_rows(normed):
    return jnp.concatenate(
        [normed[(il * 3 + ih) * 16 : (il * 3 + ih + 1) * 16] for ih in range(3) for il in range(8)], axis=0
    )


def edge(ordered, w_t):
    projected = nt(w_t, ordered)
    return jax.nn.sigmoid(projected[0:128]) * projected[128:256]


def z_parcel(values, z):
    return jnp.concatenate([values[z * 8 : z * 8 + 8, ih * 128 : ih * 128 + 128] for ih in range(3)], axis=0)


def regroup(parts, roll, bits):
    for zh in range(2):
        for ih in range(3):
            swapped = swap_lanes([parts[zh * 8 + zl][ih * 8 : ih * 8 + 8] for zl in range(8)], 16, roll, bits)
            for il in range(8):
                yield zh, ih, il, swapped[il]


def plain_row(zh, ih, il):
    return zh * 24 + ih * 8 + il


def paired_row(zh, ih, il):
    return (il >> 1) * 12 + (zh * 3 + ih) * 2 + (il & 1)


def assemble(parts, xs):
    return jnp.concatenate(
        [
            jnp.concatenate([parts(x, y * 2 + core) for y in range(4)], axis=1)
            for x in range(xs)
            for core in range(2)
        ],
        axis=0,
    )


def product_out(left, right):
    return nn(nt(left, right).astype(bf16), column_places())


def product_in(left, right, roll):
    rows = []
    for x in range(4):
        for core in range(2):
            rows += swap_lanes([left(x, y * 2 + core).astype(f32) for y in range(4)], 32, roll, (1, 2))
    turned = nt(row_places(), jnp.concatenate(rows, axis=0).astype(bf16)).astype(bf16)
    return nn(nt(turned, tight()).astype(bf16), right)


def unfold(parts, roll):
    columns = [[] for _ in range(8)]
    for ih in range(3):
        turned = jnp.concatenate([part[ih * 8 : ih * 8 + 8] for part in parts], axis=0).T
        for p in range(8):
            columns[p].append(turned[p * 16 : p * 16 + 16])
    return jnp.concatenate(swap_lanes([jnp.concatenate(part, axis=0) for part in columns], 1, roll), axis=0)


def finish(state, combined, gate, weight):
    update = nn(layer_norm(combined).astype(bf16), weight)
    return (state.astype(f32) + gate * update).astype(bf16)


def kernel(
    x_ref, w1_hbm, o1_hbm, w2_hbm, o2_hbm, t1_hbm, t2_hbm, out_ref,
    w1_ref, o1_ref, w2_ref, o2_ref, t1_ref, t2_ref,
    zs, zr, wide, narrow, rs, rr, ls, ll, ls2, ll2, c1s, c1r, c2s, c2r,
    load_sem, z_send, z_recv, r_send, r_recv, l_send, l_recv, l2_send, l2_recv, c1_send, c1_recv, c2_send, c2_recv,
):
    row, col = lax.axis_index("row"), lax.axis_index("col")
    x, zh, core = row // 4, (row // 2) % 2, row % 2
    zl, y = col // 4, col % 4
    z, p = zh * 8 + zl, y * 2 + core
    g = x * 8 + p

    def z_peer(step):
        other = lax.rem(z + step, 16)
        return other, ((x * 2 + other // 8) * 2 + core, lax.rem(other, 8) * 4 + y)

    def g_peer(step):
        dx, dy, dc = step
        other_x, other_y, other_core = lax.rem(x + dx, 4), lax.rem(y + dy, 4), lax.rem(core + dc, 2)
        return (
            other_x * 8 + other_y * 2 + other_core,
            ((other_x * 2 + zh) * 2 + other_core, zl * 4 + other_y),
        )

    barrier = pltpu.get_barrier_semaphore()
    for peer, steps in ((z_peer, Z_STEPS), (g_peer, G_STEPS)):
        for step in steps:
            pl.semaphore_signal(barrier, inc=1, device_id=peer(step)[1], device_id_type=MESH)

    loads = [
        pltpu.make_async_copy(source, target, load_sem.at[i])
        for i, (source, target) in enumerate(
            (
                (w1_hbm, w1_ref), (o1_hbm, o1_ref), (w2_hbm, w2_ref),
                (o2_hbm, o2_ref), (t1_hbm, t1_ref), (t2_hbm, t2_ref),
            )
        )
    ]
    for load in loads:
        load.start()

    sent = []

    def exchange(peer, steps, source, target, me, send, recv):
        for i, step in enumerate(steps):
            other, place = peer(step)
            copy = pltpu.make_async_remote_copy(
                src_ref=source(other), dst_ref=target.at[me], send_sem=send.at[i], recv_sem=recv.at[me],
                device_id=place, device_id_type=MESH,
            )
            copy.start()
            sent.append(copy)

    def arrive(peer, steps, source, target, me, send, recv):
        for i, step in enumerate(steps):
            other, place = peer(step)
            pltpu.make_async_remote_copy(
                src_ref=source(other), dst_ref=target.at[other], send_sem=send.at[i], recv_sem=recv.at[other],
                device_id=place, device_id_type=MESH,
            ).wait_recv()

    def triangle(n, state, w_ref, o_ref):
        normed = layer_norm(state.astype(f32)).astype(bf16)
        ordered = order_rows(normed)
        loads[2 * n].wait()

        def start_z(s):
            values = edge(ordered, w_ref[:, s * 256 : s * 256 + 256].T)
            for other in range(16):
                zs[n, s, other] = z_parcel(values, other).astype(bf16)
            if n == 0 and s == 1:
                pl.semaphore_wait(barrier, len(Z_STEPS) + len(G_STEPS))
            args = (z_peer, Z_STEPS, lambda other: zs.at[n, s, other], zr.at[n, s], z, z_send.at[n, s], z_recv.at[n, s])
            exchange(*args)
            zr[n, s, z] = zs[n, s, z]
            return args

        right_z = start_z(1)
        left_z = start_z(0)
        gate = jax.nn.sigmoid(nn(normed, w_ref[:, 512:640]))
        loads[2 * n + 1].wait()

        arrive(*right_z)
        place_row = (plain_row, paired_row)[n]
        for zh_, ih, il, rows in regroup([zr[n, 1, other].astype(f32) for other in range(16)], roll_lanes, (1, 2, 4)):
            wide[pl.ds(place_row(zh_, ih, il), 8, stride=48), :] = rows
        for c in range(8):
            rs[n, c] = wide[c * 48 : c * 48 + 48, :].astype(bf16)
        right_g = (
            g_peer, G_STEPS, lambda other: rs.at[n, lax.rem(other, 8)], rr.at[n], g, r_send.at[n], r_recv.at[n]
        )
        exchange(*right_g)
        rr[n, g] = rs[n, p]

        arrive(*left_z)
        parts = [zr[n, 0, other].astype(f32) for other in range(16)]
        if n == 0:
            for zh_, ih, il, rows in regroup(parts, roll_lanes, (1, 2, 4)):
                wide[pl.ds(plain_row(zh_, ih, il), 8, stride=48), :] = rows
            for c in range(8):
                ls[c] = wide[c * 48 : c * 48 + 48, :].astype(bf16)
            left_g = (g_peer, P_STEPS, lambda other: ls.at[lax.rem(other, 8)], ll, g, l_send, l_recv)
            exchange(*left_g)
            ll[g] = ls[p]
        else:
            narrow[...] = jnp.zeros_like(narrow)
            for zh_, ih, i, rows in regroup(parts, roll_lanes, (1,)):
                narrow[pl.ds((i >> 1) * 16 + (zh_ * 3 + ih) * 2 + (i & 1), 8, stride=64), :] = rows
            for c in range(8):
                for other in range(4):
                    start = c * 64 + other * 16
                    ls2[c, other] = narrow[start : start + 16, :].astype(bf16)
            left_g = (
                g_peer, G_STEPS, lambda other: ls2.at[lax.rem(other, 8), other // 8], ll2, g, l2_send, l2_recv
            )
            exchange(*left_g)
            ll2[g] = ls2[p, x]
        arrive(*right_g)
        rights = assemble(lambda x_, p_: rr[n, x_ * 8 + p_], 4)
        arrive(*left_g)
        if n == 0:
            total = product_out(assemble(lambda x_, p_: ll[x * 8 + p_], 1), rights)
        else:
            total = product_in(lambda x_, p_: ll2[x_ * 8 + p_], rights, roll_lanes)

        for other in range(8):
            there, far = other % 2, other // 2
            c1s[n, other] = total[there * 48 : there * 48 + 48, far * 128 : far * 128 + 128].astype(bf16)
        c1 = (g_peer, P_STEPS, lambda other: c1s.at[n, lax.rem(other, 8)], c1r.at[n], g, c1_send.at[n], c1_recv.at[n])
        exchange(*c1)
        c1r[n, g] = c1s[n, p]
        arrive(*c1)
        parts = swap_lanes([c1r[n, x * 8 + other].astype(f32) for other in range(8)], 16, roll_lanes)
        for other in range(16):
            half = other // 8
            c2s[n, other] = parts[other % 8][half * 24 : half * 24 + 24].astype(bf16)
        c2 = (z_peer, Z_STEPS, lambda other: c2s.at[n, other], c2r.at[n], z, c2_send.at[n], c2_recv.at[n])
        exchange(*c2)
        c2r[n, z] = c2s[n, z]
        arrive(*c2)
        combined = unfold([c2r[n, other].astype(f32) for other in range(16)], roll_lanes)
        return finish(state, combined, gate, o_ref[...])

    state = x_ref[...].reshape(384, 128)
    state = triangle(0, state, w1_ref, o1_ref)
    state = triangle(1, state, w2_ref, o2_ref)
    normed = layer_norm(state.astype(f32)).astype(bf16)
    loads[4].wait()
    loads[5].wait()
    hidden = nn(normed, t1_ref[...])
    mixed = (jax.nn.silu(hidden[:, :512]) * hidden[:, 512:]).astype(bf16)
    result = (state.astype(f32) + nn(mixed, t2_ref[...])).astype(bf16)
    out_ref[...] = result.reshape(8, 3, 16, 128)
    for copy in sent:
        copy.wait_send()


def body(pair_state, *weights):
    x = jnp.pad(pair_state, ((0, 0), (0, 4), (0, 0))).reshape(3, 8, 16, 128).transpose(1, 0, 2, 3)
    dma = pltpu.SemaphoreType.DMA
    out = pl.pallas_call(
        kernel,
        out_shape=jax.ShapeDtypeStruct((8, 3, 16, 128), bf16),
        in_specs=[pl.BlockSpec(memory_space=pltpu.VMEM)] + [pl.BlockSpec(memory_space=pltpu.HBM)] * 6,
        out_specs=pl.BlockSpec(memory_space=pltpu.VMEM),
        scratch_shapes=[pltpu.VMEM(weight.shape, bf16) for weight in weights]
        + [
            pltpu.VMEM((2, 2, 16, 24, 128), bf16),
            pltpu.VMEM((2, 2, 16, 24, 128), bf16),
            pltpu.VMEM((384, 128), f32),
            pltpu.VMEM((512, 128), f32),
            pltpu.VMEM((2, 8, 48, 128), bf16),
            pltpu.VMEM((2, 32, 48, 128), bf16),
            pltpu.VMEM((8, 48, 128), bf16),
            pltpu.VMEM((32, 48, 128), bf16),
            pltpu.VMEM((8, 4, 16, 128), bf16),
            pltpu.VMEM((32, 16, 128), bf16),
            pltpu.VMEM((2, 8, 48, 128), bf16),
            pltpu.VMEM((2, 32, 48, 128), bf16),
            pltpu.VMEM((2, 16, 24, 128), bf16),
            pltpu.VMEM((2, 16, 24, 128), bf16),
            dma((6,)),
            dma((2, 2, 16)), dma((2, 2, 16)),
            dma((2, 32)), dma((2, 32)),
            dma((8,)), dma((32,)),
            dma((32,)), dma((32,)),
            dma((2, 8)), dma((2, 32)),
            dma((2, 16)), dma((2, 16)),
        ],
        compiler_params=pltpu.CompilerParams(
            collective_id=0, has_side_effects=True, vmem_limit_bytes=48 * 2**20
        ),
    )(x, *weights)
    return out.transpose(1, 0, 2, 3).reshape(24, 16, 128)[:, :12]


def solution(mesh):
    placed = (P("row", "col", None), P(), P(), P(), P(), P(), P())
    return jax.shard_map(
        body, mesh=mesh, in_specs=placed, out_specs=P("row", "col", None), check_vma=False
    )
```

```python
import jax
import jax.numpy as jnp
from jax import lax
from jax.experimental import pallas as pl
from jax.experimental.pallas import tpu as pltpu
from jax.sharding import PartitionSpec as P

MESH = pl.DeviceIdType.MESH
norm_eps = 1e-05
f32 = jnp.float32
bf16 = jnp.bfloat16

Z_STEPS = (8, 7, 9, 6, 10, 5, 11, 4, 12, 3, 13, 2, 14, 1, 15)
RING = (2, 1, 3, 0)
P_STEPS = tuple((0, dy, dc) for dy in RING for dc in (1, 0) if (dy, dc) != (0, 0))
G_STEPS = tuple(
    sorted(
        ((dx, dy, dc) for dx in RING for dy in RING for dc in (1, 0) if (dx, dy, dc) != (0, 0, 0)),
        key=lambda step: -(min(step[0], 4 - step[0]) + min(step[1], 4 - step[1])),
    )
)


def roll_lanes(values, shift):
    return pltpu.roll(values, shift, 1)


def swap_lanes(parts, width, roll, bits=(1, 2, 4)):
    lane = lax.broadcasted_iota(jnp.int32, parts[0].shape, 1)
    parts = list(parts)
    for bit in bits:
        low = (lane & (bit * width)) == 0
        for a in range(len(parts)):
            if a & bit == 0:
                first, second = parts[a], parts[a | bit]
                parts[a] = jnp.where(low, first, roll(second, bit * width))
                parts[a | bit] = jnp.where(low, roll(first, 128 - bit * width), second)
    return parts


def layer_norm(values):
    centred = values - jnp.mean(values, axis=-1, keepdims=True)
    spread = jnp.mean(centred * centred, axis=-1, keepdims=True)
    return centred * lax.rsqrt(spread + norm_eps)


def nt(a, b):
    return lax.dot_general(a, b, (((1,), (1,)), ((), ())), preferred_element_type=f32)


def nn(a, b):
    return jnp.dot(a, b, preferred_element_type=f32)


def ones_where(shape, row_of):
    row = lax.broadcasted_iota(jnp.int32, shape, 0)
    column = lax.broadcasted_iota(jnp.int32, shape, 1)
    return jnp.where((row == row_of(column)) & ((column & 15) < 12), 1.0, 0.0).astype(bf16)


def column_places():
    return ones_where(
        (384, 512),
        lambda n: ((n >> 5) & 3) * 96 + (n >> 8) * 48 + ((n >> 4) & 1) * 24 + ((n >> 7) & 1) * 12 + (n & 15),
    )


def row_places():
    return ones_where((96, 128), lambda n: (n >> 6) * 48 + ((n >> 4) & 1) * 24 + ((n >> 5) & 1) * 12 + (n & 15))


def order_rows(normed):
    return jnp.concatenate(
        [normed[(il * 3 + ih) * 16 : (il * 3 + ih + 1) * 16] for ih in range(3) for il in range(8)], axis=0
    )


def edge(ordered, w_t):
    projected = nt(w_t, ordered)
    return jax.nn.sigmoid(projected[0:128]) * projected[128:256]


def z_parcel(values, z):
    return jnp.concatenate([values[z * 8 : z * 8 + 8, ih * 128 : ih * 128 + 128] for ih in range(3)], axis=0)


def regroup(parts, roll):
    for ih in range(3):
        swapped = swap_lanes([part[ih * 8 : ih * 8 + 8] for part in parts], 16, roll)
        for il in range(8):
            yield ih * 8 + il, swapped[il]


def assemble(parts):
    return jnp.concatenate(
        [
            jnp.concatenate([parts(x, y * 2 + core, zh) for y in range(4)], axis=1)
            for x in range(4)
            for core in range(2)
            for zh in range(2)
        ],
        axis=0,
    )


def slot_is_remote(from_x, from_z, x, z):
    return jnp.logical_or(from_z != z, x != from_x)


def product_out(left, right, places):
    return nn(nt(left, right).astype(bf16), places)


def product_in(left, right, places, roll):
    cores = [swap_lanes([left(y * 2 + core).astype(f32) for y in range(4)], 32, roll, (1, 2)) for core in range(2)]
    rows = jnp.concatenate([cores[core][x] for x in range(4) for core in range(2)], axis=0)
    return nn(nt(places, rows.astype(bf16)).astype(bf16), right)


def unfold(parts, roll):
    columns = [[] for _ in range(8)]
    for ih in range(3):
        turned = jnp.concatenate([part[ih * 8 : ih * 8 + 8] for part in parts], axis=0).T
        for p in range(8):
            columns[p].append(turned[p * 16 : p * 16 + 16])
    return jnp.concatenate(swap_lanes([jnp.concatenate(part, axis=0) for part in columns], 1, roll), axis=0)


def finish(state, combined, gate, weight):
    update = nn(layer_norm(combined).astype(bf16), weight)
    return (state.astype(f32) + gate * update).astype(bf16)


def kernel(
    x_hbm, w1_hbm, o1_hbm, w2_hbm, o2_hbm, t1_hbm, t2_hbm, out_ref,
    x_ref, w1_ref, o1_ref, w2_ref, o2_ref, t1_ref, t2_ref,
    block, columns, rows, zs, zr, half, wide, rs, rr, ls, ll, c1s, c1r, c2s, c2r,
    load_sem, z_send, z_recv, r_send, r_recv, l_send, l_recv, c1_send, c1_recv, c2_send, c2_recv,
):
    row, col = lax.axis_index("row"), lax.axis_index("col")
    x, zh, core = row // 4, (row // 2) % 2, row % 2
    zl, y = col // 4, col % 4
    z, p = zh * 8 + zl, y * 2 + core
    g = x * 8 + p
    far_x = zl // 2

    def z_place(at_x, at_z):
        return ((at_x * 2 + at_z // 8) * 2 + core, lax.rem(at_z, 8) * 4 + y)

    def z_peer(step):
        other = lax.rem(z + step, 16)
        return other, z_place(x, other)

    def g_peer(step):
        dx, dy, dc = step
        other_x, other_y, other_core = lax.rem(x + dx, 4), lax.rem(y + dy, 4), lax.rem(core + dc, 2)
        return (
            other_x * 8 + other_y * 2 + other_core,
            ((other_x * 2 + zh) * 2 + other_core, zl * 4 + other_y),
        )

    def load(i, source, target):
        copy = pltpu.make_async_copy(source, target, load_sem.at[i])
        copy.start()
        return copy

    first_loads = [load(0, x_hbm, x_ref), load(1, w1_hbm, w1_ref)]

    barrier = pltpu.get_barrier_semaphore()
    for step in Z_STEPS:
        pl.semaphore_signal(barrier, inc=1, device_id=z_peer(step)[1], device_id_type=MESH)
    for dx in (2, 1, 3):
        for source in range(4):
            at_z = (source // 2) * 8 + x * 2 + source % 2
            pl.semaphore_signal(
                barrier, inc=1, device_id=z_place(lax.rem(x + dx, 4), at_z), device_id_type=MESH
            )
    for step in G_STEPS:
        pl.semaphore_signal(barrier, inc=1, device_id=g_peer(step)[1], device_id_type=MESH)
    greeted = len(Z_STEPS) + len(G_STEPS) + jnp.where(far_x == x, 0, 16)

    columns[...] = column_places()
    rows[...] = row_places()
    block[...] = jnp.zeros_like(block)

    sent = []

    def exchange(peer, steps, source, target, me, send, recv):
        for i, step in enumerate(steps):
            other, place = peer(step)
            copy = pltpu.make_async_remote_copy(
                src_ref=source(other), dst_ref=target(me), send_sem=send.at[i], recv_sem=recv.at[me],
                device_id=place, device_id_type=MESH,
            )
            copy.start()
            sent.append(copy)

    def arrive(peer, steps, source, target, me, send, recv):
        for i, step in enumerate(steps):
            other, place = peer(step)
            pltpu.make_async_remote_copy(
                src_ref=source(other), dst_ref=target(other), send_sem=send.at[i], recv_sem=recv.at[other],
                device_id=place, device_id_type=MESH,
            ).wait_recv()

    def far_copy(step, target, recv):
        other = lax.rem(z + step, 16)
        return pltpu.make_async_remote_copy(
            src_ref=zs.at[1, 0, other], dst_ref=zr.at[1, 0, target], send_sem=z_send.at[1, 0, step],
            recv_sem=z_recv.at[1, 0, recv], device_id=z_place(far_x, other), device_id_type=MESH,
        )

    def triangle(n, state, w_ref, o_ref, w_load, o_load):
        normed = layer_norm(state.astype(f32)).astype(bf16)
        ordered = order_rows(normed)
        w_load.wait()

        def fill_z(s):
            values = edge(ordered, w_ref[:, s * 256 : s * 256 + 256].T)
            for other in range(16):
                zs[n, s, other] = z_parcel(values, other).astype(bf16)
            return (
                z_peer, Z_STEPS, lambda other: zs.at[n, s, other], lambda me: zr.at[n, s, me], z,
                z_send.at[n, s], z_recv.at[n, s],
            )

        right_z = fill_z(1)
        if n == 0:
            pl.semaphore_wait(barrier, greeted)
        exchange(*right_z)
        zr[n, 1, z] = zs[n, 1, z]
        left_z = fill_z(0)
        slot = x * 4 + zh * 2 + lax.rem(zl, 2)
        if n == 0:
            exchange(*left_z)
            zr[n, 0, z] = zs[n, 0, z]
        else:
            for step in Z_STEPS:
                far_copy(step, slot, slot).start()

            @pl.when(far_x != x)
            def _():
                far_copy(0, slot, slot).start()

            @pl.when(far_x == x)
            def _():
                zr[1, 0, slot] = zs[1, 0, z]

        gate = jax.nn.sigmoid(nn(normed, w_ref[:, 512:640]))

        for part in range(2):
            there = zh if part == 0 else 1 - zh
            base = there * 8
            for other in range(8):

                @pl.when(base + other != z)
                def _():
                    pltpu.make_async_remote_copy(
                        src_ref=zs.at[n, 1, other], dst_ref=zr.at[n, 1, base + other], send_sem=z_send.at[n, 1, 0],
                        recv_sem=z_recv.at[n, 1, base + other], device_id=z_place(x, base + other),
                        device_id_type=MESH,
                    ).wait_recv()

            for i, values in regroup([zr[n, 1, base + other].astype(f32) for other in range(8)], roll_lanes):
                half[pl.ds(i, 8, stride=24), :] = values
            for c in range(8):
                rs[n, part, c] = half[c * 24 : c * 24 + 24, :].astype(bf16)
            exchange(
                g_peer, G_STEPS, lambda other: rs.at[n, part, lax.rem(other, 8)], lambda me: rr.at[n, there, me], g,
                r_send.at[n, part], r_recv.at[n, there],
            )
            rr[n, there, g] = rs[n, part, p]

        if n == 0:
            arrive(*left_z)
            parts = [[zr[n, 0, zh_ * 8 + zl_].astype(f32) for zl_ in range(8)] for zh_ in range(2)]
        else:
            for other in range(16):
                at_z = ((other // 2) % 2) * 8 + x * 2 + other % 2

                @pl.when(slot_is_remote(other // 4, at_z, x, z))
                def _():
                    far_copy(0, other, other).wait_recv()

            parts = [
                [zr[n, 0, x_ * 4 + zh_ * 2 + zlo].astype(f32) for x_ in range(4) for zlo in range(2)]
                for zh_ in range(2)
            ]
        for zh_ in range(2):
            for i, values in regroup(parts[zh_], roll_lanes):
                wide[pl.ds(zh_ * 24 + i, 8, stride=48), :] = values
        for c in range(8):
            ls[n, c] = wide[c * 48 : c * 48 + 48, :].astype(bf16)
        left_g = (
            g_peer, P_STEPS, lambda other: ls.at[n, lax.rem(other, 8)], lambda me: ll.at[n, me], g,
            l_send.at[n], l_recv.at[n],
        )
        exchange(*left_g)
        ll[n, g] = ls[n, p]
        for there in range(2):
            arrive(
                g_peer, G_STEPS, lambda other: rs.at[n, 0, lax.rem(other, 8)], lambda me: rr.at[n, there, me], g,
                r_send.at[n, 0], r_recv.at[n, there],
            )
        rights = assemble(lambda x_, p_, zh_: rr[n, zh_, x_ * 8 + p_])
        arrive(*left_g)
        if n == 0:
            lefts = jnp.concatenate(
                [
                    jnp.concatenate([ll[n, x * 8 + y_ * 2 + core_] for y_ in range(4)], axis=1)
                    for core_ in range(2)
                ],
                axis=0,
            )
            total = product_out(lefts, rights, columns[...])
        else:
            total = product_in(lambda p_: ll[n, x * 8 + p_], rights, rows[...], roll_lanes)

        for other in range(8):
            there, far = other % 2, other // 2
            c1s[n, other] = total[there * 48 : there * 48 + 48, far * 128 : far * 128 + 128].astype(bf16)
        c1 = (
            g_peer, P_STEPS, lambda other: c1s.at[n, lax.rem(other, 8)], lambda me: c1r.at[n, me], g,
            c1_send.at[n], c1_recv.at[n],
        )
        exchange(*c1)
        c1r[n, g] = c1s[n, p]
        arrive(*c1)
        parts = swap_lanes([c1r[n, x * 8 + other].astype(f32) for other in range(8)], 16, roll_lanes)
        for other in range(16):
            start = (other // 8) * 24
            c2s[n, other] = parts[other % 8][start : start + 24].astype(bf16)
        c2 = (
            z_peer, Z_STEPS, lambda other: c2s.at[n, other], lambda me: c2r.at[n, me], z,
            c2_send.at[n], c2_recv.at[n],
        )
        exchange(*c2)
        c2r[n, z] = c2s[n, z]
        o_load.wait()
        arrive(*c2)
        combined = unfold([c2r[n, other].astype(f32) for other in range(16)], roll_lanes)
        return finish(state, combined, gate, o_ref[...])

    first_loads[0].wait()
    for k in range(12):
        for ih in range(3):
            block[pl.ds(ih * 16 + k, 8, stride=48), :] = x_ref[k, ih * 8 : ih * 8 + 8].astype(f32)
    later = [
        load(2 + i, source, target)
        for i, (source, target) in enumerate(
            ((o1_hbm, o1_ref), (w2_hbm, w2_ref), (o2_hbm, o2_ref), (t1_hbm, t1_ref), (t2_hbm, t2_ref))
        )
    ]
    state = block[...].astype(bf16)
    state = triangle(0, state, w1_ref, o1_ref, first_loads[1], later[0])
    state = triangle(1, state, w2_ref, o2_ref, later[1], later[2])
    normed = layer_norm(state.astype(f32)).astype(bf16)
    later[3].wait()
    later[4].wait()
    hidden = nn(normed, t1_ref[...])
    mixed = (jax.nn.silu(hidden[:, :512]) * hidden[:, 512:]).astype(bf16)
    block[...] = state.astype(f32) + nn(mixed, t2_ref[...])
    for k in range(12):
        out_ref[k] = jnp.concatenate(
            [block[pl.ds(ih * 16 + k, 8, stride=48), :] for ih in range(3)], axis=0
        ).astype(bf16)
    for copy in sent:
        copy.wait_send()
    for step in Z_STEPS:
        far_copy(step, 0, 0).wait_send()

    @pl.when(far_x != x)
    def _():
        far_copy(0, 0, 0).wait_send()


def body(pair_state, *weights):
    dma = pltpu.SemaphoreType.DMA
    out = pl.pallas_call(
        kernel,
        out_shape=jax.ShapeDtypeStruct((12, 24, 128), bf16),
        in_specs=[pl.BlockSpec(memory_space=pltpu.HBM)] * 7,
        out_specs=pl.BlockSpec(memory_space=pltpu.VMEM),
        scratch_shapes=[pltpu.VMEM((12, 24, 128), bf16)]
        + [pltpu.VMEM(weight.shape, bf16) for weight in weights]
        + [
            pltpu.VMEM((384, 128), f32),
            pltpu.VMEM((384, 512), bf16),
            pltpu.VMEM((96, 128), bf16),
            pltpu.VMEM((2, 2, 16, 24, 128), bf16),
            pltpu.VMEM((2, 2, 16, 24, 128), bf16),
            pltpu.VMEM((192, 128), f32),
            pltpu.VMEM((384, 128), f32),
            pltpu.VMEM((2, 2, 8, 24, 128), bf16),
            pltpu.VMEM((2, 2, 32, 24, 128), bf16),
            pltpu.VMEM((2, 8, 48, 128), bf16),
            pltpu.VMEM((2, 32, 48, 128), bf16),
            pltpu.VMEM((2, 8, 48, 128), bf16),
            pltpu.VMEM((2, 32, 48, 128), bf16),
            pltpu.VMEM((2, 16, 24, 128), bf16),
            pltpu.VMEM((2, 16, 24, 128), bf16),
            dma((7,)),
            dma((2, 2, 16)), dma((2, 2, 16)),
            dma((2, 2, 32)), dma((2, 2, 32)),
            dma((2, 8)), dma((2, 32)),
            dma((2, 8)), dma((2, 32)),
            dma((2, 16)), dma((2, 16)),
        ],
        compiler_params=pltpu.CompilerParams(
            collective_id=0, has_side_effects=True, vmem_limit_bytes=60 * 2**20
        ),
    )(pair_state.transpose(1, 0, 2), *weights)
    return out.transpose(1, 0, 2)


def solution(mesh):
    placed = (P("row", "col", None), P(), P(), P(), P(), P(), P())
    return jax.shard_map(
        body, mesh=mesh, in_specs=placed, out_specs=P("row", "col", None), check_vma=False
    )
```

```python
import jax
import jax.numpy as jnp
from jax import lax
from jax.experimental import pallas as pl
from jax.experimental.pallas import tpu as pltpu
from jax.sharding import PartitionSpec as P

MESH = pl.DeviceIdType.MESH
norm_eps = 1e-05
f32 = jnp.float32
bf16 = jnp.bfloat16

Z_STEPS = (8, 7, 9, 6, 10, 5, 11, 4, 12, 3, 13, 2, 14, 1, 15)
RING = (2, 1, 3, 0)
P_STEPS = tuple((0, dy, dc) for dy in RING for dc in (1, 0) if (dy, dc) != (0, 0))
G_STEPS = tuple(
    sorted(
        ((dx, dy, dc) for dx in RING for dy in RING for dc in (1, 0) if (dx, dy, dc) != (0, 0, 0)),
        key=lambda step: -(min(step[0], 4 - step[0]) + min(step[1], 4 - step[1])),
    )
)


def roll_lanes(values, shift):
    return pltpu.roll(values, shift, 1)


def swap_lanes(parts, width, roll, bits=(1, 2, 4)):
    lane = lax.broadcasted_iota(jnp.int32, parts[0].shape, 1)
    parts = list(parts)
    for bit in bits:
        low = (lane & (bit * width)) == 0
        for a in range(len(parts)):
            if a & bit == 0:
                first, second = parts[a], parts[a | bit]
                parts[a] = jnp.where(low, first, roll(second, bit * width))
                parts[a | bit] = jnp.where(low, roll(first, 128 - bit * width), second)
    return parts


def layer_norm(values):
    centred = values - jnp.mean(values, axis=-1, keepdims=True)
    spread = jnp.mean(centred * centred, axis=-1, keepdims=True)
    return centred * lax.rsqrt(spread + norm_eps)


def nt(a, b):
    return lax.dot_general(a, b, (((1,), (1,)), ((), ())), preferred_element_type=f32)


def nn(a, b):
    return jnp.dot(a, b, preferred_element_type=f32)


def ones_where(shape, row_of):
    row = lax.broadcasted_iota(jnp.int32, shape, 0)
    column = lax.broadcasted_iota(jnp.int32, shape, 1)
    return jnp.where((row == row_of(column)) & ((column & 15) < 12), 1.0, 0.0).astype(bf16)


def column_places():
    return ones_where(
        (384, 512),
        lambda n: ((n >> 5) & 3) * 96 + (n >> 8) * 48 + ((n >> 4) & 1) * 24 + ((n >> 7) & 1) * 12 + (n & 15),
    )


def row_places():
    return ones_where((96, 128), lambda n: (n >> 6) * 48 + ((n >> 4) & 1) * 24 + ((n >> 5) & 1) * 12 + (n & 15))


def order_rows(normed):
    return jnp.concatenate(
        [normed[(il * 3 + ih) * 16 : (il * 3 + ih + 1) * 16] for ih in range(3) for il in range(8)], axis=0
    )


def edge(ordered, w_t):
    projected = nt(w_t, ordered)
    return jax.nn.sigmoid(projected[0:128]) * projected[128:256]


def z_parcel(values, z):
    return jnp.concatenate([values[z * 8 : z * 8 + 8, ih * 128 : ih * 128 + 128] for ih in range(3)], axis=0)


def regroup(parts, roll):
    for ih in range(3):
        swapped = swap_lanes([part[ih * 8 : ih * 8 + 8] for part in parts], 16, roll)
        for il in range(8):
            yield ih * 8 + il, swapped[il]


def assemble(parts):
    return jnp.concatenate(
        [
            jnp.concatenate([parts(x, y * 2 + core) for y in range(4)], axis=1)
            for x in range(4)
            for core in range(2)
        ],
        axis=0,
    )


def product_out(left, right, places):
    return nn(nt(left, right).astype(bf16), places)


def product_in(left, right, places, roll):
    cores = [swap_lanes([left(y * 2 + core).astype(f32) for y in range(4)], 32, roll, (1, 2)) for core in range(2)]
    rows = jnp.concatenate([cores[core][x] for x in range(4) for core in range(2)], axis=0)
    return nn(nt(places, rows.astype(bf16)).astype(bf16), right)


def unfold(parts, roll):
    columns = [[] for _ in range(8)]
    for ih in range(3):
        turned = jnp.concatenate([part[ih * 8 : ih * 8 + 8] for part in parts], axis=0).T
        for p in range(8):
            columns[p].append(turned[p * 16 : p * 16 + 16])
    return jnp.concatenate(swap_lanes([jnp.concatenate(part, axis=0) for part in columns], 1, roll), axis=0)


def finish(state, combined, gate, weight):
    update = nn(layer_norm(combined).astype(bf16), weight)
    return (state.astype(f32) + gate * update).astype(bf16)


def kernel(
    x_hbm, w1_hbm, o1_hbm, w2_hbm, o2_hbm, t1_hbm, t2_hbm, out_ref,
    x_ref, w1_ref, o1_ref, w2_ref, o2_ref, t1_ref, t2_ref,
    block, columns, rows, zs, zr, wide, rs, rr, ls, ll, c1s, c1r, c2s, c2r,
    load_sem, z_send, z_recv, r_send, r_recv, l_send, l_recv, c1_send, c1_recv, c2_send, c2_recv,
):
    row, col = lax.axis_index("row"), lax.axis_index("col")
    x, zh, core = row // 4, (row // 2) % 2, row % 2
    zl, y = col // 4, col % 4
    z, p = zh * 8 + zl, y * 2 + core
    g = x * 8 + p
    far_x = zl // 2
    from_own = far_x == x

    def z_place(at_x, at_z):
        return ((at_x * 2 + at_z // 8) * 2 + core, lax.rem(at_z, 8) * 4 + y)

    def z_peer(step):
        other = lax.rem(z + step, 16)
        return other, z_place(x, other)

    def g_peer(step):
        dx, dy, dc = step
        other_x, other_y, other_core = lax.rem(x + dx, 4), lax.rem(y + dy, 4), lax.rem(core + dc, 2)
        return (
            other_x * 8 + other_y * 2 + other_core,
            ((other_x * 2 + zh) * 2 + other_core, zl * 4 + other_y),
        )

    def load(i, source, target):
        copy = pltpu.make_async_copy(source, target, load_sem.at[i])
        copy.start()
        return copy

    first_loads = [load(0, x_hbm, x_ref), load(1, w1_hbm, w1_ref)]

    barrier = pltpu.get_barrier_semaphore()
    for step in Z_STEPS:
        pl.semaphore_signal(barrier, inc=1, device_id=z_peer(step)[1], device_id_type=MESH)
    for dx in (2, 1, 3):
        for source in range(4):
            at_z = (source // 2) * 8 + x * 2 + source % 2
            pl.semaphore_signal(
                barrier, inc=1, device_id=z_place(lax.rem(x + dx, 4), at_z), device_id_type=MESH
            )
    for step in G_STEPS:
        pl.semaphore_signal(barrier, inc=1, device_id=g_peer(step)[1], device_id_type=MESH)
    greeted = len(Z_STEPS) + len(G_STEPS) + jnp.where(from_own, 0, 16)

    columns[...] = column_places()
    rows[...] = row_places()
    block[...] = jnp.zeros_like(block)

    sent = []

    def exchange(peer, steps, source, target, me, send, recv):
        for step in steps:
            other, place = peer(step)
            pltpu.make_async_remote_copy(
                src_ref=source(other), dst_ref=target.at[me], send_sem=send, recv_sem=recv,
                device_id=place, device_id_type=MESH,
            ).start()
        sent.append((target, len(steps), send))

    def all_bytes(target, count, sem):
        blocks = target.at[pl.ds(0, count)]
        return pltpu.make_async_copy(blocks, blocks, sem)

    def arrive(peer, steps, source, target, me, send, recv):
        all_bytes(target, len(steps), recv).wait()

    def far_copy(step):
        other = lax.rem(z + step, 16)
        pltpu.make_async_remote_copy(
            src_ref=zs.at[1, 0, other], dst_ref=zr.at[1, 0, x * 4 + zh * 2 + lax.rem(zl, 2)],
            send_sem=z_send.at[1, 0], recv_sem=z_recv.at[1, 0],
            device_id=z_place(far_x, other), device_id_type=MESH,
        ).start()

    later = []

    def triangle(n, state, w_ref, o_ref):
        normed = layer_norm(state.astype(f32)).astype(bf16)
        ordered = order_rows(normed)
        (first_loads[1] if n == 0 else later[1]).wait()

        def fill_z(s):
            values = edge(ordered, w_ref[:, s * 256 : s * 256 + 256].T)
            for other in range(16):
                zs[n, s, other] = z_parcel(values, other).astype(bf16)
            return (
                z_peer, Z_STEPS, lambda other: zs.at[n, s, other], zr.at[n, s], z,
                z_send.at[n, s], z_recv.at[n, s],
            )

        right_z = fill_z(1)
        if n == 0:
            pl.semaphore_wait(barrier, greeted)
        exchange(*right_z)
        zr[n, 1, z] = zs[n, 1, z]
        left_z = fill_z(0)
        slot = x * 4 + zh * 2 + lax.rem(zl, 2)
        if n == 0:
            exchange(*left_z)
            zr[n, 0, z] = zs[n, 0, z]
            for i, (source, target) in enumerate(
                ((o1_hbm, o1_ref), (w2_hbm, w2_ref), (o2_hbm, o2_ref), (t1_hbm, t1_ref), (t2_hbm, t2_ref))
            ):
                later.append(load(2 + i, source, target))
        else:
            for step in Z_STEPS:
                far_copy(step)

            @pl.when(jnp.logical_not(from_own))
            def _():
                far_copy(0)

            @pl.when(from_own)
            def _():
                zr[1, 0, slot] = zs[1, 0, z]

        gate = jax.nn.sigmoid(nn(normed, w_ref[:, 512:640]))

        arrive(*right_z)
        for zh_ in range(2):
            for i, values in regroup([zr[n, 1, zh_ * 8 + zl_].astype(f32) for zl_ in range(8)], roll_lanes):
                wide[pl.ds(zh_ * 24 + i, 8, stride=48), :] = values
        for c in range(8):
            rs[n, c] = wide[c * 48 : c * 48 + 48, :].astype(bf16)
        right_g = (
            g_peer, G_STEPS, lambda other: rs.at[n, lax.rem(other, 8)], rr.at[n], g,
            r_send.at[n], r_recv.at[n],
        )
        exchange(*right_g)
        rr[n, g] = rs[n, p]

        if n == 0:
            arrive(*left_z)
            parts = [[zr[n, 0, zh_ * 8 + zl_].astype(f32) for zl_ in range(8)] for zh_ in range(2)]
        else:
            @pl.when(from_own)
            def _():
                all_bytes(zr.at[1, 0], 15, z_recv.at[1, 0]).wait()

            @pl.when(jnp.logical_not(from_own))
            def _():
                all_bytes(zr.at[1, 0], 16, z_recv.at[1, 0]).wait()

            parts = [
                [zr[n, 0, x_ * 4 + zh_ * 2 + zlo].astype(f32) for x_ in range(4) for zlo in range(2)]
                for zh_ in range(2)
            ]
        for zh_ in range(2):
            for i, values in regroup(parts[zh_], roll_lanes):
                wide[pl.ds(zh_ * 24 + i, 8, stride=48), :] = values
        for c in range(8):
            ls[n, c] = wide[c * 48 : c * 48 + 48, :].astype(bf16)
        left_g = (
            g_peer, P_STEPS, lambda other: ls.at[n, lax.rem(other, 8)], ll.at[n], g,
            l_send.at[n], l_recv.at[n],
        )
        exchange(*left_g)
        ll[n, g] = ls[n, p]
        arrive(*right_g)
        rights = assemble(lambda x_, p_: rr[n, x_ * 8 + p_])
        arrive(*left_g)
        if n == 0:
            lefts = jnp.concatenate(
                [
                    jnp.concatenate([ll[n, x * 8 + y_ * 2 + core_] for y_ in range(4)], axis=1)
                    for core_ in range(2)
                ],
                axis=0,
            )
            total = product_out(lefts, rights, columns[...])
        else:
            total = product_in(lambda p_: ll[n, x * 8 + p_], rights, rows[...], roll_lanes)

        for other in range(8):
            there, far = other % 2, other // 2
            c1s[n, other] = total[there * 48 : there * 48 + 48, far * 128 : far * 128 + 128].astype(bf16)
        c1 = (
            g_peer, P_STEPS, lambda other: c1s.at[n, lax.rem(other, 8)], c1r.at[n], g,
            c1_send.at[n], c1_recv.at[n],
        )
        exchange(*c1)
        c1r[n, g] = c1s[n, p]
        arrive(*c1)
        parts = swap_lanes([c1r[n, x * 8 + other].astype(f32) for other in range(8)], 16, roll_lanes)
        for other in range(16):
            start = (other // 8) * 24
            c2s[n, other] = parts[other % 8][start : start + 24].astype(bf16)
        c2 = (
            z_peer, Z_STEPS, lambda other: c2s.at[n, other], c2r.at[n], z,
            c2_send.at[n], c2_recv.at[n],
        )
        exchange(*c2)
        c2r[n, z] = c2s[n, z]
        later[2 * n].wait()
        arrive(*c2)
        combined = unfold([c2r[n, other].astype(f32) for other in range(16)], roll_lanes)
        return finish(state, combined, gate, o_ref[...])

    first_loads[0].wait()
    for k in range(12):
        for ih in range(3):
            block[pl.ds(ih * 16 + k, 8, stride=48), :] = x_ref[k, ih * 8 : ih * 8 + 8].astype(f32)
    state = block[...].astype(bf16)
    state = triangle(0, state, w1_ref, o1_ref)
    state = triangle(1, state, w2_ref, o2_ref)
    normed = layer_norm(state.astype(f32)).astype(bf16)
    later[3].wait()
    later[4].wait()
    hidden = nn(normed, t1_ref[...])
    mixed = (jax.nn.silu(hidden[:, :512]) * hidden[:, 512:]).astype(bf16)
    block[...] = state.astype(f32) + nn(mixed, t2_ref[...])
    for k in range(12):
        out_ref[k] = jnp.concatenate(
            [block[pl.ds(ih * 16 + k, 8, stride=48), :] for ih in range(3)], axis=0
        ).astype(bf16)
    for target, count, send in sent:
        all_bytes(target, count, send).wait()

    @pl.when(from_own)
    def _():
        all_bytes(zs.at[1, 0], 15, z_send.at[1, 0]).wait()

    @pl.when(jnp.logical_not(from_own))
    def _():
        all_bytes(zs.at[1, 0], 16, z_send.at[1, 0]).wait()


def body(pair_state, *weights):
    dma = pltpu.SemaphoreType.DMA
    out = pl.pallas_call(
        kernel,
        out_shape=jax.ShapeDtypeStruct((12, 24, 128), bf16),
        in_specs=[pl.BlockSpec(memory_space=pltpu.HBM)] * 7,
        out_specs=pl.BlockSpec(memory_space=pltpu.VMEM),
        scratch_shapes=[pltpu.VMEM((12, 24, 128), bf16)]
        + [pltpu.VMEM(weight.shape, bf16) for weight in weights]
        + [
            pltpu.VMEM((384, 128), f32),
            pltpu.VMEM((384, 512), bf16),
            pltpu.VMEM((96, 128), bf16),
            pltpu.VMEM((2, 2, 16, 24, 128), bf16),
            pltpu.VMEM((2, 2, 16, 24, 128), bf16),
            pltpu.VMEM((384, 128), f32),
            pltpu.VMEM((2, 8, 48, 128), bf16),
            pltpu.VMEM((2, 32, 48, 128), bf16),
            pltpu.VMEM((2, 8, 48, 128), bf16),
            pltpu.VMEM((2, 32, 48, 128), bf16),
            pltpu.VMEM((2, 8, 48, 128), bf16),
            pltpu.VMEM((2, 32, 48, 128), bf16),
            pltpu.VMEM((2, 16, 24, 128), bf16),
            pltpu.VMEM((2, 16, 24, 128), bf16),
            dma((7,)),
            dma((2, 2)), dma((2, 2)),
            dma((2,)), dma((2,)),
            dma((2,)), dma((2,)),
            dma((2,)), dma((2,)),
            dma((2,)), dma((2,)),
        ],
        compiler_params=pltpu.CompilerParams(
            collective_id=0, has_side_effects=True, vmem_limit_bytes=60 * 2**20
        ),
    )(pair_state.transpose(1, 0, 2), *weights)
    return out.transpose(1, 0, 2)


def solution(mesh):
    placed = (P("row", "col", None), P(), P(), P(), P(), P(), P())
    return jax.shard_map(
        body, mesh=mesh, in_specs=placed, out_specs=P("row", "col", None), check_vma=False
    )
```

```python
import jax
import jax.numpy as jnp
from jax import lax
from jax.experimental import pallas as pl
from jax.experimental.pallas import tpu as pltpu
from jax.sharding import PartitionSpec as P

MESH = pl.DeviceIdType.MESH
norm_eps = 1e-05
f32 = jnp.float32
bf16 = jnp.bfloat16

Z_STEPS = (8, 7, 9, 6, 10, 5, 11, 4, 12, 3, 13, 2, 14, 1, 15)


def far_first(steps):
    def hops(step):
        return min(step[0], 4 - step[0]) + min(step[1], 4 - step[1]) + step[2]

    return tuple(sorted(steps, key=lambda step: (-hops(step), -min(step[1], 4 - step[1]), step[0], step[1])))


P_STEPS = far_first((0, dy, dc) for dy in range(4) for dc in range(2) if (dy, dc) != (0, 0))
G_STEPS = far_first(
    (dx, dy, dc) for dx in range(4) for dy in range(4) for dc in range(2) if (dx, dy, dc) != (0, 0, 0)
)


def roll_lanes(values, shift):
    return pltpu.roll(values, shift, 1)


def swap_lanes(parts, width, roll, bits=(1, 2, 4)):
    lane = lax.broadcasted_iota(jnp.int32, parts[0].shape, 1)
    parts = list(parts)
    for bit in bits:
        low = (lane & (bit * width)) == 0
        for a in range(len(parts)):
            if a & bit == 0:
                first, second = parts[a], parts[a | bit]
                parts[a] = jnp.where(low, first, roll(second, bit * width))
                parts[a | bit] = jnp.where(low, roll(first, 128 - bit * width), second)
    return parts


def layer_norm(values):
    centred = values - jnp.mean(values, axis=-1, keepdims=True)
    spread = jnp.mean(centred * centred, axis=-1, keepdims=True)
    return centred * lax.rsqrt(spread + norm_eps)


def nt(a, b):
    return lax.dot_general(a, b, (((1,), (1,)), ((), ())), preferred_element_type=f32)


def nn(a, b):
    return jnp.dot(a, b, preferred_element_type=f32)


def ones_where(shape, row_of):
    row = lax.broadcasted_iota(jnp.int32, shape, 0)
    column = lax.broadcasted_iota(jnp.int32, shape, 1)
    return jnp.where((row == row_of(column)) & ((column & 15) < 12), 1.0, 0.0).astype(bf16)


def column_places():
    return ones_where(
        (384, 512),
        lambda n: ((n >> 5) & 3) * 96 + (n >> 8) * 48 + ((n >> 4) & 1) * 24 + ((n >> 7) & 1) * 12 + (n & 15),
    )


def row_places():
    return ones_where((96, 128), lambda n: (n >> 6) * 48 + ((n >> 4) & 1) * 24 + ((n >> 5) & 1) * 12 + (n & 15))


def order_rows(normed):
    return jnp.concatenate(
        [normed[(il * 3 + ih) * 16 : (il * 3 + ih + 1) * 16] for ih in range(3) for il in range(8)], axis=0
    )


def edge(ordered, w_t):
    projected = nt(w_t, ordered)
    return jax.nn.sigmoid(projected[0:128]) * projected[128:256]


def z_parcel(values, z):
    return jnp.concatenate([values[z * 8 : z * 8 + 8, ih * 128 : ih * 128 + 128] for ih in range(3)], axis=0)


def regroup(parts, roll):
    for ih in range(3):
        swapped = swap_lanes([part[ih * 8 : ih * 8 + 8] for part in parts], 16, roll)
        for il in range(8):
            yield ih * 8 + il, swapped[il]


def pack_rows(rows, roll):
    spare = (lax.broadcasted_iota(jnp.int32, rows[0].shape, 1) & 15) >= 12
    packed = list(rows[:40])
    for third in range(3):
        for a in range(8):
            b = third * 8 + a
            packed[b] = jnp.where(spare, roll(rows[40 + a], 12 - 4 * third), packed[b])
    return packed


def unpack_rows(packed, roll):
    count = packed.shape[0]
    packed = packed.astype(f32)
    thirds = [
        roll(packed[:, third * 8 : third * 8 + 8].reshape(count * 8, 128), 116 + 4 * third) for third in range(3)
    ]
    inside = lax.broadcasted_iota(jnp.int32, thirds[0].shape, 1) & 15
    last = jnp.where(inside < 4, thirds[0], jnp.where(inside < 8, thirds[1], thirds[2]))
    return jnp.concatenate([packed, last.reshape(count, 8, 128)], axis=1).astype(bf16)


def assemble(parts):
    return jnp.concatenate(
        [
            jnp.concatenate([parts(x, y * 2 + core) for y in range(4)], axis=1)
            for x in range(4)
            for core in range(2)
        ],
        axis=0,
    )


def product_out(left, right, places):
    return nn(nt(left, right).astype(bf16), places)


def product_in(left, right, places, roll):
    cores = [swap_lanes([left(y * 2 + core).astype(f32) for y in range(4)], 32, roll, (1, 2)) for core in range(2)]
    rows = jnp.concatenate([cores[core][x] for x in range(4) for core in range(2)], axis=0)
    return nn(nt(places, rows.astype(bf16)).astype(bf16), right)


def unfold(parts, roll):
    columns = [[] for _ in range(8)]
    for ih in range(3):
        turned = jnp.concatenate([part[ih * 8 : ih * 8 + 8] for part in parts], axis=0).T
        for p in range(8):
            columns[p].append(turned[p * 16 : p * 16 + 16])
    return jnp.concatenate(swap_lanes([jnp.concatenate(part, axis=0) for part in columns], 1, roll), axis=0)


def finish(state, combined, gate, weight):
    update = nn(layer_norm(combined).astype(bf16), weight)
    return (state.astype(f32) + gate * update).astype(bf16)


def kernel(
    x_hbm, w1_hbm, o1_hbm, w2_hbm, o2_hbm, t1_hbm, t2_hbm, out_ref,
    x_ref, w1_ref, o1_ref, w2_ref, o2_ref, t1_ref, t2_ref,
    block, columns, rows, zs, zr, wide, narrow, rs, rr, ls, ll, c1s, c1r, c2s, c2r,
    load_sem, z_send, z_recv, r_send, r_recv, l_send, l_recv, c1_send, c1_recv, c2_send, c2_recv,
):
    row, col = lax.axis_index("row"), lax.axis_index("col")
    x, zh, core = row // 4, (row // 2) % 2, row % 2
    zl, y = col // 4, col % 4
    z, p = zh * 8 + zl, y * 2 + core
    g = x * 8 + p
    far_x = zl // 2
    from_own = far_x == x

    def z_place(at_x, at_z):
        return ((at_x * 2 + at_z // 8) * 2 + core, lax.rem(at_z, 8) * 4 + y)

    def z_peer(step):
        other = lax.rem(z + step, 16)
        return other, z_place(x, other)

    def g_peer(step):
        dx, dy, dc = step
        other_x, other_y, other_core = lax.rem(x + dx, 4), lax.rem(y + dy, 4), lax.rem(core + dc, 2)
        return (
            other_x * 8 + other_y * 2 + other_core,
            ((other_x * 2 + zh) * 2 + other_core, zl * 4 + other_y),
        )

    def load(i, source, target):
        copy = pltpu.make_async_copy(source, target, load_sem.at[i])
        copy.start()
        return copy

    first_loads = [load(0, x_hbm, x_ref), load(1, w1_hbm, w1_ref)]

    barrier = pltpu.get_barrier_semaphore()
    for step in Z_STEPS:
        pl.semaphore_signal(barrier, inc=1, device_id=z_peer(step)[1], device_id_type=MESH)
    for dx in (2, 1, 3):
        for source in range(4):
            at_z = (source // 2) * 8 + x * 2 + source % 2
            pl.semaphore_signal(
                barrier, inc=1, device_id=z_place(lax.rem(x + dx, 4), at_z), device_id_type=MESH
            )
    for step in G_STEPS:
        pl.semaphore_signal(barrier, inc=1, device_id=g_peer(step)[1], device_id_type=MESH)
    greeted = len(Z_STEPS) + len(G_STEPS) + jnp.where(from_own, 0, 16)

    columns[...] = column_places()
    rows[...] = row_places()
    block[...] = jnp.zeros_like(block)

    sent = []

    def exchange(peer, steps, source, target, me, send, recv):
        for step in steps:
            other, place = peer(step)
            pltpu.make_async_remote_copy(
                src_ref=source(other), dst_ref=target.at[me], send_sem=send, recv_sem=recv,
                device_id=place, device_id_type=MESH,
            ).start()
        sent.append((target, len(steps), send))

    def all_bytes(target, count, sem):
        blocks = target.at[pl.ds(0, count)]
        return pltpu.make_async_copy(blocks, blocks, sem)

    def arrive(peer, steps, source, target, me, send, recv):
        all_bytes(target, len(steps), recv).wait()

    def far_copy(step):
        other = lax.rem(z + step, 16)
        pltpu.make_async_remote_copy(
            src_ref=zs.at[1, 0, other], dst_ref=zr.at[1, 0, x * 4 + zh * 2 + lax.rem(zl, 2)],
            send_sem=z_send.at[1, 0], recv_sem=z_recv.at[1, 0],
            device_id=z_place(far_x, other), device_id_type=MESH,
        ).start()

    later = []

    def triangle(n, state, w_ref, o_ref):
        normed = layer_norm(state.astype(f32)).astype(bf16)
        ordered = order_rows(normed)
        (first_loads[1] if n == 0 else later[1]).wait()

        def fill_z(s):
            values = edge(ordered, w_ref[:, s * 256 : s * 256 + 256].T)
            for other in range(16):
                zs[n, s, other] = z_parcel(values, other).astype(bf16)
            return (
                z_peer, Z_STEPS, lambda other: zs.at[n, s, other], zr.at[n, s], z,
                z_send.at[n, s], z_recv.at[n, s],
            )

        right_z = fill_z(1)
        if n == 0:
            pl.semaphore_wait(barrier, greeted)
        exchange(*right_z)
        zr[n, 1, z] = zs[n, 1, z]
        left_z = fill_z(0)
        slot = x * 4 + zh * 2 + lax.rem(zl, 2)
        if n == 0:
            exchange(*left_z)
            zr[n, 0, z] = zs[n, 0, z]
            for i, (source, target) in enumerate(
                ((o1_hbm, o1_ref), (w2_hbm, w2_ref), (o2_hbm, o2_ref), (t1_hbm, t1_ref), (t2_hbm, t2_ref))
            ):
                later.append(load(2 + i, source, target))
        else:
            for step in Z_STEPS:
                far_copy(step)

            @pl.when(jnp.logical_not(from_own))
            def _():
                far_copy(0)

            @pl.when(from_own)
            def _():
                zr[1, 0, slot] = zs[1, 0, z]

        gate = jax.nn.sigmoid(nn(normed, w_ref[:, 512:640]))

        arrive(*right_z)
        values = [
            value
            for zh_ in range(2)
            for _, value in regroup([zr[n, 1, zh_ * 8 + zl_].astype(f32) for zl_ in range(8)], roll_lanes)
        ]
        for i, value in enumerate(pack_rows(values, roll_lanes)):
            narrow[pl.ds(i, 8, stride=40), :] = value
        for c in range(8):
            rs[n, c] = narrow[c * 40 : c * 40 + 40, :].astype(bf16)
        right_g = (
            g_peer, G_STEPS, lambda other: rs.at[n, lax.rem(other, 8)], rr.at[n], g,
            r_send.at[n], r_recv.at[n],
        )
        exchange(*right_g)
        rr[n, g] = rs[n, p]

        if n == 0:
            arrive(*left_z)
            parts = [[zr[n, 0, zh_ * 8 + zl_].astype(f32) for zl_ in range(8)] for zh_ in range(2)]
        else:
            @pl.when(from_own)
            def _():
                all_bytes(zr.at[1, 0], 15, z_recv.at[1, 0]).wait()

            @pl.when(jnp.logical_not(from_own))
            def _():
                all_bytes(zr.at[1, 0], 16, z_recv.at[1, 0]).wait()

            parts = [
                [zr[n, 0, x_ * 4 + zh_ * 2 + zlo].astype(f32) for x_ in range(4) for zlo in range(2)]
                for zh_ in range(2)
            ]
        for zh_ in range(2):
            for i, values in regroup(parts[zh_], roll_lanes):
                wide[pl.ds(zh_ * 24 + i, 8, stride=48), :] = values
        for c in range(8):
            ls[n, c] = wide[c * 48 : c * 48 + 48, :].astype(bf16)
        left_g = (
            g_peer, P_STEPS, lambda other: ls.at[n, lax.rem(other, 8)], ll.at[n], g,
            l_send.at[n], l_recv.at[n],
        )
        exchange(*left_g)
        ll[n, g] = ls[n, p]
        arrive(*right_g)
        unpacked = unpack_rows(rr[n], roll_lanes)
        rights = assemble(lambda x_, p_: unpacked[x_ * 8 + p_])
        arrive(*left_g)
        if n == 0:
            lefts = jnp.concatenate(
                [
                    jnp.concatenate([ll[n, x * 8 + y_ * 2 + core_] for y_ in range(4)], axis=1)
                    for core_ in range(2)
                ],
                axis=0,
            )
            total = product_out(lefts, rights, columns[...])
        else:
            total = product_in(lambda p_: ll[n, x * 8 + p_], rights, rows[...], roll_lanes)

        for other in range(8):
            there, far = other % 2, other // 2
            c1s[n, other] = total[there * 48 : there * 48 + 48, far * 128 : far * 128 + 128].astype(bf16)
        c1 = (
            g_peer, P_STEPS, lambda other: c1s.at[n, lax.rem(other, 8)], c1r.at[n], g,
            c1_send.at[n], c1_recv.at[n],
        )
        exchange(*c1)
        c1r[n, g] = c1s[n, p]
        arrive(*c1)
        parts = swap_lanes([c1r[n, x * 8 + other].astype(f32) for other in range(8)], 16, roll_lanes)
        for other in range(16):
            start = (other // 8) * 24
            c2s[n, other] = parts[other % 8][start : start + 24].astype(bf16)
        c2 = (
            z_peer, Z_STEPS, lambda other: c2s.at[n, other], c2r.at[n], z,
            c2_send.at[n], c2_recv.at[n],
        )
        exchange(*c2)
        c2r[n, z] = c2s[n, z]
        later[2 * n].wait()
        arrive(*c2)
        combined = unfold([c2r[n, other].astype(f32) for other in range(16)], roll_lanes)
        return finish(state, combined, gate, o_ref[...])

    first_loads[0].wait()
    for k in range(12):
        for ih in range(3):
            block[pl.ds(ih * 16 + k, 8, stride=48), :] = x_ref[k, ih * 8 : ih * 8 + 8].astype(f32)
    state = block[...].astype(bf16)
    state = triangle(0, state, w1_ref, o1_ref)
    state = triangle(1, state, w2_ref, o2_ref)
    normed = layer_norm(state.astype(f32)).astype(bf16)
    later[3].wait()
    later[4].wait()
    hidden = nn(normed, t1_ref[...])
    mixed = (jax.nn.silu(hidden[:, :512]) * hidden[:, 512:]).astype(bf16)
    block[...] = state.astype(f32) + nn(mixed, t2_ref[...])
    for k in range(12):
        out_ref[k] = jnp.concatenate(
            [block[pl.ds(ih * 16 + k, 8, stride=48), :] for ih in range(3)], axis=0
        ).astype(bf16)
    for target, count, send in sent:
        all_bytes(target, count, send).wait()

    @pl.when(from_own)
    def _():
        all_bytes(zs.at[1, 0], 15, z_send.at[1, 0]).wait()

    @pl.when(jnp.logical_not(from_own))
    def _():
        all_bytes(zs.at[1, 0], 16, z_send.at[1, 0]).wait()


def body(pair_state, *weights):
    dma = pltpu.SemaphoreType.DMA
    out = pl.pallas_call(
        kernel,
        out_shape=jax.ShapeDtypeStruct((12, 24, 128), bf16),
        in_specs=[pl.BlockSpec(memory_space=pltpu.HBM)] * 7,
        out_specs=pl.BlockSpec(memory_space=pltpu.VMEM),
        scratch_shapes=[pltpu.VMEM((12, 24, 128), bf16)]
        + [pltpu.VMEM(weight.shape, bf16) for weight in weights]
        + [
            pltpu.VMEM((384, 128), f32),
            pltpu.VMEM((384, 512), bf16),
            pltpu.VMEM((96, 128), bf16),
            pltpu.VMEM((2, 2, 16, 24, 128), bf16),
            pltpu.VMEM((2, 2, 16, 24, 128), bf16),
            pltpu.VMEM((384, 128), f32),
            pltpu.VMEM((320, 128), f32),
            pltpu.VMEM((2, 8, 40, 128), bf16),
            pltpu.VMEM((2, 32, 40, 128), bf16),
            pltpu.VMEM((2, 8, 48, 128), bf16),
            pltpu.VMEM((2, 32, 48, 128), bf16),
            pltpu.VMEM((2, 8, 48, 128), bf16),
            pltpu.VMEM((2, 32, 48, 128), bf16),
            pltpu.VMEM((2, 16, 24, 128), bf16),
            pltpu.VMEM((2, 16, 24, 128), bf16),
            dma((7,)),
            dma((2, 2)), dma((2, 2)),
            dma((2,)), dma((2,)),
            dma((2,)), dma((2,)),
            dma((2,)), dma((2,)),
            dma((2,)), dma((2,)),
        ],
        compiler_params=pltpu.CompilerParams(
            collective_id=0, has_side_effects=True, vmem_limit_bytes=60 * 2**20
        ),
    )(pair_state.transpose(1, 0, 2), *weights)
    return out.transpose(1, 0, 2)


def solution(mesh):
    placed = (P("row", "col", None), P(), P(), P(), P(), P(), P())
    return jax.shard_map(
        body, mesh=mesh, in_specs=placed, out_specs=P("row", "col", None), check_vma=False
    )
```

```python
import jax
import jax.numpy as jnp
from jax import lax
from jax.experimental import pallas as pl
from jax.experimental.pallas import tpu as pltpu
from jax.sharding import PartitionSpec as P

MESH = pl.DeviceIdType.MESH
norm_eps = 1e-05
f32 = jnp.float32
bf16 = jnp.bfloat16

Z_STEPS = (8, 7, 9, 6, 10, 5, 11, 4, 12, 3, 13, 2, 14, 1, 15)


def far_first(steps):
    def hops(step):
        return min(step[0], 4 - step[0]) + min(step[1], 4 - step[1]) + step[2]

    return tuple(sorted(steps, key=lambda step: (-hops(step), -min(step[1], 4 - step[1]), step[0], step[1])))


P_STEPS = far_first((0, dy, dc) for dy in range(4) for dc in range(2) if (dy, dc) != (0, 0))
G_STEPS = far_first(
    (dx, dy, dc) for dx in range(4) for dy in range(4) for dc in range(2) if (dx, dy, dc) != (0, 0, 0)
)


def roll_lanes(values, shift):
    return pltpu.roll(values, shift, 1)


def swap_lanes(parts, width, roll, bits=(1, 2, 4)):
    lane = lax.broadcasted_iota(jnp.int32, parts[0].shape, 1)
    parts = list(parts)
    for bit in bits:
        low = (lane & (bit * width)) == 0
        for a in range(len(parts)):
            if a & bit == 0:
                first, second = parts[a], parts[a | bit]
                parts[a] = jnp.where(low, first, roll(second, bit * width))
                parts[a | bit] = jnp.where(low, roll(first, 128 - bit * width), second)
    return parts


def layer_norm(values):
    centred = values - jnp.mean(values, axis=-1, keepdims=True)
    spread = jnp.mean(centred * centred, axis=-1, keepdims=True)
    return centred * lax.rsqrt(spread + norm_eps)


def nt(a, b):
    return lax.dot_general(a, b, (((1,), (1,)), ((), ())), preferred_element_type=f32)


def nn(a, b):
    return jnp.dot(a, b, preferred_element_type=f32)


def ones_where(shape, row_of):
    row = lax.broadcasted_iota(jnp.int32, shape, 0)
    column = lax.broadcasted_iota(jnp.int32, shape, 1)
    return jnp.where((row == row_of(column)) & ((column & 15) < 12), 1.0, 0.0).astype(bf16)


def column_places():
    return ones_where(
        (384, 512),
        lambda n: ((n >> 5) & 3) * 96 + (n >> 8) * 48 + ((n >> 4) & 1) * 24 + ((n >> 7) & 1) * 12 + (n & 15),
    )


def row_places():
    return ones_where((96, 128), lambda n: (n >> 6) * 48 + ((n >> 4) & 1) * 24 + ((n >> 5) & 1) * 12 + (n & 15))


def order_rows(normed):
    return jnp.concatenate(
        [normed[(il * 3 + ih) * 16 : (il * 3 + ih + 1) * 16] for ih in range(3) for il in range(8)], axis=0
    )


def edge(ordered, w_t):
    projected = nt(w_t, ordered)
    return jax.nn.sigmoid(projected[0:128]) * projected[128:256]


def z_parcel(values, z, groups=3):
    return jnp.concatenate([values[z * 8 : z * 8 + 8, ih * 128 : ih * 128 + 128] for ih in range(groups)], axis=0)


def lend_lanes(right, left, roll):
    spare = (lax.broadcasted_iota(jnp.int32, (128, 128), 1) & 15) >= 12
    return jnp.concatenate(
        [
            jnp.where(spare, roll(left[:, 256:384], 12 - 4 * ih), right[:, ih * 128 : ih * 128 + 128])
            for ih in range(3)
        ],
        axis=1,
    )


def lent_rows(right, roll):
    thirds = [roll(right[ih * 8 : ih * 8 + 8], 116 + 4 * ih) for ih in range(3)]
    inside = lax.broadcasted_iota(jnp.int32, (8, 128), 1) & 15
    last = jnp.where(inside < 12, thirds[2], 0.0)
    return jnp.where(inside < 4, thirds[0], jnp.where(inside < 8, thirds[1], last))


def regroup(parts, roll):
    for ih in range(3):
        swapped = swap_lanes([part[ih * 8 : ih * 8 + 8] for part in parts], 16, roll)
        for il in range(8):
            yield ih * 8 + il, swapped[il]


def pack_rows(rows, roll):
    spare = (lax.broadcasted_iota(jnp.int32, rows[0].shape, 1) & 15) >= 12
    packed = list(rows[:40])
    for third in range(3):
        for a in range(8):
            b = third * 8 + a
            packed[b] = jnp.where(spare, roll(rows[40 + a], 12 - 4 * third), packed[b])
    return packed


def unpack_rows(packed, roll):
    count = packed.shape[0]
    packed = packed.astype(f32)
    thirds = [
        roll(packed[:, third * 8 : third * 8 + 8].reshape(count * 8, 128), 116 + 4 * third) for third in range(3)
    ]
    inside = lax.broadcasted_iota(jnp.int32, thirds[0].shape, 1) & 15
    last = jnp.where(inside < 4, thirds[0], jnp.where(inside < 8, thirds[1], thirds[2]))
    return jnp.concatenate([packed, last.reshape(count, 8, 128)], axis=1).astype(bf16)


def assemble(parts):
    return jnp.concatenate(
        [
            jnp.concatenate([parts(x, y * 2 + core) for y in range(4)], axis=1)
            for x in range(4)
            for core in range(2)
        ],
        axis=0,
    )


def product_out(left, right, places):
    return nn(nt(left, right).astype(bf16), places)


def product_in(left, right, places, roll):
    cores = [swap_lanes([left(y * 2 + core).astype(f32) for y in range(4)], 32, roll, (1, 2)) for core in range(2)]
    rows = jnp.concatenate([cores[core][x] for x in range(4) for core in range(2)], axis=0)
    return nn(nt(places, rows.astype(bf16)).astype(bf16), right)


def unfold(parts, roll):
    columns = [[] for _ in range(8)]
    for ih in range(3):
        turned = jnp.concatenate([part[ih * 8 : ih * 8 + 8] for part in parts], axis=0).T
        for p in range(8):
            columns[p].append(turned[p * 16 : p * 16 + 16])
    return jnp.concatenate(swap_lanes([jnp.concatenate(part, axis=0) for part in columns], 1, roll), axis=0)


def finish(state, combined, gate, weight):
    update = nn(layer_norm(combined).astype(bf16), weight)
    return (state.astype(f32) + gate * update).astype(bf16)


def kernel(
    x_hbm, w1_hbm, o1_hbm, w2_hbm, o2_hbm, t1_hbm, t2_hbm, out_ref,
    x_ref, w1_ref, o1_ref, w2_ref, o2_ref, t1_ref, t2_ref,
    block, columns, rows, zs, zr, short_s, short_r, wide, narrow, rs, rr, ls, ll, c1s, c1r, c2s, c2r,
    load_sem, z_send, z_recv, r_send, r_recv, l_send, l_recv, c1_send, c1_recv, c2_send, c2_recv,
):
    row, col = lax.axis_index("row"), lax.axis_index("col")
    x, zh, core = row // 4, (row // 2) % 2, row % 2
    zl, y = col // 4, col % 4
    z, p = zh * 8 + zl, y * 2 + core
    g = x * 8 + p
    far_x = zl // 2
    from_own = far_x == x

    def z_place(at_x, at_z):
        return ((at_x * 2 + at_z // 8) * 2 + core, lax.rem(at_z, 8) * 4 + y)

    def z_peer(step):
        other = lax.rem(z + step, 16)
        return other, z_place(x, other)

    def g_peer(step):
        dx, dy, dc = step
        other_x, other_y, other_core = lax.rem(x + dx, 4), lax.rem(y + dy, 4), lax.rem(core + dc, 2)
        return (
            other_x * 8 + other_y * 2 + other_core,
            ((other_x * 2 + zh) * 2 + other_core, zl * 4 + other_y),
        )

    def load(i, source, target):
        copy = pltpu.make_async_copy(source, target, load_sem.at[i])
        copy.start()
        return copy

    first_loads = [load(0, x_hbm, x_ref), load(1, w1_hbm, w1_ref)]

    barrier = pltpu.get_barrier_semaphore()
    for step in Z_STEPS:
        pl.semaphore_signal(barrier, inc=1, device_id=z_peer(step)[1], device_id_type=MESH)
    for dx in (2, 1, 3):
        for source in range(4):
            at_z = (source // 2) * 8 + x * 2 + source % 2
            pl.semaphore_signal(
                barrier, inc=1, device_id=z_place(lax.rem(x + dx, 4), at_z), device_id_type=MESH
            )
    for step in G_STEPS:
        pl.semaphore_signal(barrier, inc=1, device_id=g_peer(step)[1], device_id_type=MESH)
    greeted = len(Z_STEPS) + len(G_STEPS) + jnp.where(from_own, 0, 16)

    columns[...] = column_places()
    rows[...] = row_places()
    block[...] = jnp.zeros_like(block)

    sent = []

    def exchange(peer, steps, source, target, me, send, recv):
        for step in steps:
            other, place = peer(step)
            pltpu.make_async_remote_copy(
                src_ref=source(other), dst_ref=target.at[me], send_sem=send, recv_sem=recv,
                device_id=place, device_id_type=MESH,
            ).start()
        sent.append((target, len(steps), send))

    def all_bytes(target, count, sem):
        blocks = target.at[pl.ds(0, count)]
        return pltpu.make_async_copy(blocks, blocks, sem)

    def arrive(peer, steps, source, target, me, send, recv):
        all_bytes(target, len(steps), recv).wait()

    def far_copy(step):
        other = lax.rem(z + step, 16)
        pltpu.make_async_remote_copy(
            src_ref=zs.at[1, 0, other], dst_ref=zr.at[1, 0, x * 4 + zh * 2 + lax.rem(zl, 2)],
            send_sem=z_send.at[1, 0], recv_sem=z_recv.at[1, 0],
            device_id=z_place(far_x, other), device_id_type=MESH,
        ).start()

    later = []

    def triangle(n, state, w_ref, o_ref):
        normed = layer_norm(state.astype(f32)).astype(bf16)
        ordered = order_rows(normed)
        (first_loads[1] if n == 0 else later[1]).wait()

        def edges(s):
            return edge(ordered, w_ref[:, s * 256 : s * 256 + 256].T)

        right = edges(1)
        if n == 0:
            left = edges(0)
            right = lend_lanes(right, left, roll_lanes)
        for other in range(16):
            zs[n, 1, other] = z_parcel(right, other).astype(bf16)
        right_z = (
            z_peer, Z_STEPS, lambda other: zs.at[n, 1, other], zr.at[n, 1], z, z_send.at[n, 1], z_recv.at[n, 1]
        )
        if n == 0:
            pl.semaphore_wait(barrier, greeted)
        exchange(*right_z)
        zr[n, 1, z] = zs[n, 1, z]
        slot = x * 4 + zh * 2 + lax.rem(zl, 2)
        if n == 0:
            for other in range(16):
                short_s[other] = z_parcel(left, other, 2).astype(bf16)
            left_z = (
                z_peer, Z_STEPS, lambda other: short_s.at[other], short_r, z, z_send.at[n, 0], z_recv.at[n, 0]
            )
            exchange(*left_z)
            short_r[z] = short_s[z]
            for i, (source, target) in enumerate(
                ((o1_hbm, o1_ref), (w2_hbm, w2_ref), (o2_hbm, o2_ref), (t1_hbm, t1_ref), (t2_hbm, t2_ref))
            ):
                later.append(load(2 + i, source, target))
        else:
            left = edges(0)
            for other in range(16):
                zs[n, 0, other] = z_parcel(left, other).astype(bf16)
            for step in Z_STEPS:
                far_copy(step)

            @pl.when(jnp.logical_not(from_own))
            def _():
                far_copy(0)

            @pl.when(from_own)
            def _():
                zr[1, 0, slot] = zs[1, 0, z]

        gate = jax.nn.sigmoid(nn(normed, w_ref[:, 512:640]))

        arrive(*right_z)
        values = [
            value
            for zh_ in range(2)
            for _, value in regroup([zr[n, 1, zh_ * 8 + zl_].astype(f32) for zl_ in range(8)], roll_lanes)
        ]
        for i, value in enumerate(pack_rows(values, roll_lanes)):
            narrow[pl.ds(i, 8, stride=40), :] = value
        for c in range(8):
            rs[n, c] = narrow[c * 40 : c * 40 + 40, :].astype(bf16)
        right_g = (
            g_peer, G_STEPS, lambda other: rs.at[n, lax.rem(other, 8)], rr.at[n], g,
            r_send.at[n], r_recv.at[n],
        )
        exchange(*right_g)
        rr[n, g] = rs[n, p]

        if n == 0:
            arrive(*left_z)
            parts = [
                [
                    jnp.concatenate(
                        [
                            short_r[zh_ * 8 + zl_].astype(f32),
                            lent_rows(zr[n, 1, zh_ * 8 + zl_].astype(f32), roll_lanes),
                        ],
                        axis=0,
                    )
                    for zl_ in range(8)
                ]
                for zh_ in range(2)
            ]
        else:
            @pl.when(from_own)
            def _():
                all_bytes(zr.at[1, 0], 15, z_recv.at[1, 0]).wait()

            @pl.when(jnp.logical_not(from_own))
            def _():
                all_bytes(zr.at[1, 0], 16, z_recv.at[1, 0]).wait()

            parts = [
                [zr[n, 0, x_ * 4 + zh_ * 2 + zlo].astype(f32) for x_ in range(4) for zlo in range(2)]
                for zh_ in range(2)
            ]
        for zh_ in range(2):
            for i, values in regroup(parts[zh_], roll_lanes):
                wide[pl.ds(zh_ * 24 + i, 8, stride=48), :] = values
        for c in range(8):
            ls[n, c] = wide[c * 48 : c * 48 + 48, :].astype(bf16)
        left_g = (
            g_peer, P_STEPS, lambda other: ls.at[n, lax.rem(other, 8)], ll.at[n], g,
            l_send.at[n], l_recv.at[n],
        )
        exchange(*left_g)
        ll[n, g] = ls[n, p]
        arrive(*right_g)
        unpacked = unpack_rows(rr[n], roll_lanes)
        rights = assemble(lambda x_, p_: unpacked[x_ * 8 + p_])
        arrive(*left_g)
        if n == 0:
            lefts = jnp.concatenate(
                [
                    jnp.concatenate([ll[n, x * 8 + y_ * 2 + core_] for y_ in range(4)], axis=1)
                    for core_ in range(2)
                ],
                axis=0,
            )
            total = product_out(lefts, rights, columns[...])
        else:
            total = product_in(lambda p_: ll[n, x * 8 + p_], rights, rows[...], roll_lanes)

        for other in range(8):
            there, far = other % 2, other // 2
            c1s[n, other] = total[there * 48 : there * 48 + 48, far * 128 : far * 128 + 128].astype(bf16)
        c1 = (
            g_peer, P_STEPS, lambda other: c1s.at[n, lax.rem(other, 8)], c1r.at[n], g,
            c1_send.at[n], c1_recv.at[n],
        )
        exchange(*c1)
        c1r[n, g] = c1s[n, p]
        arrive(*c1)
        parts = swap_lanes([c1r[n, x * 8 + other].astype(f32) for other in range(8)], 16, roll_lanes)
        for other in range(16):
            start = (other // 8) * 24
            c2s[n, other] = parts[other % 8][start : start + 24].astype(bf16)
        c2 = (
            z_peer, Z_STEPS, lambda other: c2s.at[n, other], c2r.at[n], z,
            c2_send.at[n], c2_recv.at[n],
        )
        exchange(*c2)
        c2r[n, z] = c2s[n, z]
        later[2 * n].wait()
        arrive(*c2)
        combined = unfold([c2r[n, other].astype(f32) for other in range(16)], roll_lanes)
        return finish(state, combined, gate, o_ref[...])

    first_loads[0].wait()
    for k in range(12):
        for ih in range(3):
            block[pl.ds(ih * 16 + k, 8, stride=48), :] = x_ref[k, ih * 8 : ih * 8 + 8].astype(f32)
    state = block[...].astype(bf16)
    state = triangle(0, state, w1_ref, o1_ref)
    state = triangle(1, state, w2_ref, o2_ref)
    normed = layer_norm(state.astype(f32)).astype(bf16)
    later[3].wait()
    later[4].wait()
    hidden = nn(normed, t1_ref[...])
    mixed = (jax.nn.silu(hidden[:, :512]) * hidden[:, 512:]).astype(bf16)
    block[...] = state.astype(f32) + nn(mixed, t2_ref[...])
    for k in range(12):
        out_ref[k] = jnp.concatenate(
            [block[pl.ds(ih * 16 + k, 8, stride=48), :] for ih in range(3)], axis=0
        ).astype(bf16)
    for target, count, send in sent:
        all_bytes(target, count, send).wait()

    @pl.when(from_own)
    def _():
        all_bytes(zs.at[1, 0], 15, z_send.at[1, 0]).wait()

    @pl.when(jnp.logical_not(from_own))
    def _():
        all_bytes(zs.at[1, 0], 16, z_send.at[1, 0]).wait()


def body(pair_state, *weights):
    dma = pltpu.SemaphoreType.DMA
    out = pl.pallas_call(
        kernel,
        out_shape=jax.ShapeDtypeStruct((12, 24, 128), bf16),
        in_specs=[pl.BlockSpec(memory_space=pltpu.HBM)] * 7,
        out_specs=pl.BlockSpec(memory_space=pltpu.VMEM),
        scratch_shapes=[pltpu.VMEM((12, 24, 128), bf16)]
        + [pltpu.VMEM(weight.shape, bf16) for weight in weights]
        + [
            pltpu.VMEM((384, 128), f32),
            pltpu.VMEM((384, 512), bf16),
            pltpu.VMEM((96, 128), bf16),
            pltpu.VMEM((2, 2, 16, 24, 128), bf16),
            pltpu.VMEM((2, 2, 16, 24, 128), bf16),
            pltpu.VMEM((16, 16, 128), bf16),
            pltpu.VMEM((16, 16, 128), bf16),
            pltpu.VMEM((384, 128), f32),
            pltpu.VMEM((320, 128), f32),
            pltpu.VMEM((2, 8, 40, 128), bf16),
            pltpu.VMEM((2, 32, 40, 128), bf16),
            pltpu.VMEM((2, 8, 48, 128), bf16),
            pltpu.VMEM((2, 32, 48, 128), bf16),
            pltpu.VMEM((2, 8, 48, 128), bf16),
            pltpu.VMEM((2, 32, 48, 128), bf16),
            pltpu.VMEM((2, 16, 24, 128), bf16),
            pltpu.VMEM((2, 16, 24, 128), bf16),
            dma((7,)),
            dma((2, 2)), dma((2, 2)),
            dma((2,)), dma((2,)),
            dma((2,)), dma((2,)),
            dma((2,)), dma((2,)),
            dma((2,)), dma((2,)),
        ],
        compiler_params=pltpu.CompilerParams(
            collective_id=0, has_side_effects=True, vmem_limit_bytes=60 * 2**20
        ),
    )(pair_state.transpose(1, 0, 2), *weights)
    return out.transpose(1, 0, 2)


def solution(mesh):
    placed = (P("row", "col", None), P(), P(), P(), P(), P(), P())
    return jax.shard_map(
        body, mesh=mesh, in_specs=placed, out_specs=P("row", "col", None), check_vma=False
    )
```

```python
import jax
import jax.numpy as jnp
from jax import lax
from jax.experimental import pallas as pl
from jax.experimental.pallas import tpu as pltpu
from jax.sharding import PartitionSpec as P

MESH = pl.DeviceIdType.MESH
norm_eps = 1e-05
f32 = jnp.float32
bf16 = jnp.bfloat16

Z_STEPS = (8, 7, 9, 6, 10, 5, 11, 4, 12, 3, 13, 2, 14, 1, 15)


def far_first(steps):
    def hops(step):
        return min(step[0], 4 - step[0]) + min(step[1], 4 - step[1]) + step[2]

    return tuple(sorted(steps, key=lambda step: (-hops(step), -min(step[1], 4 - step[1]), step[0], step[1])))


P_STEPS = far_first((0, dy, dc) for dy in range(4) for dc in range(2) if (dy, dc) != (0, 0))
G_STEPS = far_first(
    (dx, dy, dc) for dx in range(4) for dy in range(4) for dc in range(2) if (dx, dy, dc) != (0, 0, 0)
)


def roll_lanes(values, shift):
    return pltpu.roll(values, shift, 1)


def swap_lanes(parts, width, roll, bits=(1, 2, 4)):
    lane = lax.broadcasted_iota(jnp.int32, parts[0].shape, 1)
    parts = list(parts)
    for bit in bits:
        low = (lane & (bit * width)) == 0
        for a in range(len(parts)):
            if a & bit == 0:
                first, second = parts[a], parts[a | bit]
                parts[a] = jnp.where(low, first, roll(second, bit * width))
                parts[a | bit] = jnp.where(low, roll(first, 128 - bit * width), second)
    return parts


def layer_norm(values):
    centred = values - jnp.mean(values, axis=-1, keepdims=True)
    spread = jnp.mean(centred * centred, axis=-1, keepdims=True)
    return centred * lax.rsqrt(spread + norm_eps)


def nt(a, b):
    return lax.dot_general(a, b, (((1,), (1,)), ((), ())), preferred_element_type=f32)


def nn(a, b):
    return jnp.dot(a, b, preferred_element_type=f32)


def ones_where(shape, row_of):
    row = lax.broadcasted_iota(jnp.int32, shape, 0)
    column = lax.broadcasted_iota(jnp.int32, shape, 1)
    return jnp.where((row == row_of(column)) & ((column & 15) < 12), 1.0, 0.0).astype(bf16)


def column_places():
    return ones_where(
        (384, 512),
        lambda n: ((n >> 5) & 3) * 96 + (n >> 8) * 48 + ((n >> 4) & 1) * 24 + ((n >> 7) & 1) * 12 + (n & 15),
    )


def row_places():
    return ones_where((96, 128), lambda n: (n >> 6) * 48 + ((n >> 4) & 1) * 24 + ((n >> 5) & 1) * 12 + (n & 15))


def order_rows(normed):
    return jnp.concatenate(
        [normed[(il * 3 + ih) * 16 : (il * 3 + ih + 1) * 16] for ih in range(3) for il in range(8)], axis=0
    )


def edge(ordered, w_t):
    projected = nt(w_t, ordered)
    return jax.nn.sigmoid(projected[0:128]) * projected[128:256]


def z_parcel(values, z, groups=3):
    return jnp.concatenate([values[z * 8 : z * 8 + 8, ih * 128 : ih * 128 + 128] for ih in range(groups)], axis=0)


def lend_lanes(right, left, roll):
    spare = (lax.broadcasted_iota(jnp.int32, (128, 128), 1) & 15) >= 12
    return jnp.concatenate(
        [
            jnp.where(spare, roll(left[:, 256:384], 12 - 4 * ih), right[:, ih * 128 : ih * 128 + 128])
            for ih in range(3)
        ],
        axis=1,
    )


def lent_rows(right, roll):
    thirds = [roll(right[ih * 8 : ih * 8 + 8], 116 + 4 * ih) for ih in range(3)]
    inside = lax.broadcasted_iota(jnp.int32, (8, 128), 1) & 15
    last = jnp.where(inside < 12, thirds[2], 0.0)
    return jnp.where(inside < 4, thirds[0], jnp.where(inside < 8, thirds[1], last))


def regroup(parts, roll):
    for ih in range(3):
        swapped = swap_lanes([part[ih * 8 : ih * 8 + 8] for part in parts], 16, roll)
        for il in range(8):
            yield ih * 8 + il, swapped[il]


def pack_rows(rows, roll):
    spare = (lax.broadcasted_iota(jnp.int32, rows[0].shape, 1) & 15) >= 12
    packed = list(rows[:40])
    for third in range(3):
        for a in range(8):
            b = third * 8 + a
            packed[b] = jnp.where(spare, roll(rows[40 + a], 12 - 4 * third), packed[b])
    return packed


def unpack_rows(packed, roll):
    count = packed.shape[0]
    packed = packed.astype(f32)
    thirds = [
        roll(packed[:, third * 8 : third * 8 + 8].reshape(count * 8, 128), 116 + 4 * third) for third in range(3)
    ]
    inside = lax.broadcasted_iota(jnp.int32, thirds[0].shape, 1) & 15
    last = jnp.where(inside < 4, thirds[0], jnp.where(inside < 8, thirds[1], thirds[2]))
    return jnp.concatenate([packed, last.reshape(count, 8, 128)], axis=1).astype(bf16)


def assemble(parts):
    return jnp.concatenate(
        [
            jnp.concatenate([parts(x, y * 2 + core) for y in range(4)], axis=1)
            for x in range(4)
            for core in range(2)
        ],
        axis=0,
    )


def product_out(left, right, places):
    return nn(nt(left, right).astype(bf16), places)


def product_in(left, right, places, roll):
    cores = [swap_lanes([left(y * 2 + core).astype(f32) for y in range(4)], 32, roll, (1, 2)) for core in range(2)]
    rows = jnp.concatenate([cores[core][x] for x in range(4) for core in range(2)], axis=0)
    return nn(nt(places, rows.astype(bf16)).astype(bf16), right)


def unfold(parts, roll):
    columns = [[] for _ in range(8)]
    for ih in range(3):
        turned = jnp.concatenate([part[ih * 8 : ih * 8 + 8] for part in parts], axis=0).T
        for p in range(8):
            columns[p].append(turned[p * 16 : p * 16 + 16])
    return jnp.concatenate(swap_lanes([jnp.concatenate(part, axis=0) for part in columns], 1, roll), axis=0)


def finish(state, combined, gate, weight):
    update = nn(layer_norm(combined).astype(bf16), weight)
    return (state.astype(f32) + gate * update).astype(bf16)


def kernel(
    x_hbm, w1_hbm, o1_hbm, w2_hbm, o2_hbm, t1_hbm, t2_hbm, out_ref,
    x_ref, w1_ref, o1_ref, w2_ref, o2_ref, t1_ref, t2_ref,
    block, columns, rows, zs, zr, short_s, short_r, wide, narrow, rs, rr, ls, ll, c1s, c1r, c2s, c2r,
    load_sem, z_send, z_recv, r_send, r_recv, l_send, l_recv, c1_send, c1_recv, c2_send, c2_recv,
):
    row, col = lax.axis_index("row"), lax.axis_index("col")
    x, zh, core = row // 4, (row // 2) % 2, row % 2
    zl, y = col // 4, col % 4
    z, p = zh * 8 + zl, y * 2 + core
    g = x * 8 + p
    far_x = zl // 2
    from_own = far_x == x

    def z_place(at_x, at_z):
        return ((at_x * 2 + at_z // 8) * 2 + core, lax.rem(at_z, 8) * 4 + y)

    def z_peer(step):
        other = lax.rem(z + step, 16)
        return other, z_place(x, other)

    def g_peer(step):
        dx, dy, dc = step
        other_x, other_y, other_core = lax.rem(x + dx, 4), lax.rem(y + dy, 4), lax.rem(core + dc, 2)
        return (
            other_x * 8 + other_y * 2 + other_core,
            ((other_x * 2 + zh) * 2 + other_core, zl * 4 + other_y),
        )

    def load(i, source, target):
        copy = pltpu.make_async_copy(source, target, load_sem.at[i])
        copy.start()
        return copy

    first_loads = [load(0, x_hbm, x_ref), load(1, w1_hbm, w1_ref)]

    barrier = pltpu.get_barrier_semaphore()
    for step in Z_STEPS:
        pl.semaphore_signal(barrier, inc=1, device_id=z_peer(step)[1], device_id_type=MESH)
    for dx in (2, 1, 3):
        for source in range(4):
            at_z = (source // 2) * 8 + x * 2 + source % 2
            pl.semaphore_signal(
                barrier, inc=1, device_id=z_place(lax.rem(x + dx, 4), at_z), device_id_type=MESH
            )
    for step in G_STEPS:
        pl.semaphore_signal(barrier, inc=1, device_id=g_peer(step)[1], device_id_type=MESH)
    greeted = len(Z_STEPS) + len(G_STEPS) + jnp.where(from_own, 0, 16)

    columns[...] = column_places()
    rows[...] = row_places()
    block[...] = jnp.zeros_like(block)

    sent = []

    def exchange(peer, steps, source, target, me, send, recv):
        for step in steps:
            other, place = peer(step)
            pltpu.make_async_remote_copy(
                src_ref=source(other), dst_ref=target.at[me], send_sem=send, recv_sem=recv,
                device_id=place, device_id_type=MESH,
            ).start()
        sent.append((target, len(steps), send))

    def all_bytes(target, count, sem):
        blocks = target.at[pl.ds(0, count)]
        return pltpu.make_async_copy(blocks, blocks, sem)

    def arrive(peer, steps, source, target, me, send, recv):
        all_bytes(target, len(steps), recv).wait()

    def far_copy(step):
        other = lax.rem(z + step, 16)
        pltpu.make_async_remote_copy(
            src_ref=zs.at[1, 0, other], dst_ref=zr.at[1, 0, x * 4 + zh * 2 + lax.rem(zl, 2)],
            send_sem=z_send.at[1, 0], recv_sem=z_recv.at[1, 0],
            device_id=z_place(far_x, other), device_id_type=MESH,
        ).start()

    later = []

    def triangle(n, state, w_ref, o_ref):
        normed = layer_norm(state.astype(f32)).astype(bf16)
        ordered = order_rows(normed)
        (first_loads[1] if n == 0 else later[1]).wait()

        def edges(s):
            return edge(ordered, w_ref[:, s * 256 : s * 256 + 256].T)

        right = edges(1)
        if n == 0:
            left = edges(0)
            right = lend_lanes(right, left, roll_lanes)
        for other in range(16):
            zs[n, 1, other] = z_parcel(right, other).astype(bf16)
        right_z = (
            z_peer, Z_STEPS, lambda other: zs.at[n, 1, other], zr.at[n, 1], z, z_send.at[n, 1], z_recv.at[n, 1]
        )
        if n == 0:
            pl.semaphore_wait(barrier, greeted)
        exchange(*right_z)
        zr[n, 1, z] = zs[n, 1, z]
        slot = x * 4 + zh * 2 + lax.rem(zl, 2)
        if n == 0:
            for other in range(16):
                short_s[other] = z_parcel(left, other, 2).astype(bf16)
            left_z = (
                z_peer, Z_STEPS, lambda other: short_s.at[other], short_r, z, z_send.at[n, 0], z_recv.at[n, 0]
            )
            exchange(*left_z)
            short_r[z] = short_s[z]
            for i, (source, target) in enumerate(
                ((o1_hbm, o1_ref), (w2_hbm, w2_ref), (o2_hbm, o2_ref), (t1_hbm, t1_ref), (t2_hbm, t2_ref))
            ):
                later.append(load(2 + i, source, target))
        else:
            left = edges(0)
            for other in range(16):
                zs[n, 0, other] = z_parcel(left, other).astype(bf16)
            for step in Z_STEPS:
                far_copy(step)

            @pl.when(jnp.logical_not(from_own))
            def _():
                far_copy(0)

            @pl.when(from_own)
            def _():
                zr[1, 0, slot] = zs[1, 0, z]

        gate = jax.nn.sigmoid(nn(normed, w_ref[:, 512:640]))

        arrive(*right_z)
        values = [
            value
            for zh_ in range(2)
            for _, value in regroup([zr[n, 1, zh_ * 8 + zl_].astype(f32) for zl_ in range(8)], roll_lanes)
        ]
        for i, value in enumerate(pack_rows(values, roll_lanes)):
            narrow[pl.ds(i, 8, stride=40), :] = value
        for c in range(8):
            rs[n, c] = narrow[c * 40 : c * 40 + 40, :].astype(bf16)
        right_g = (
            g_peer, G_STEPS, lambda other: rs.at[n, lax.rem(other, 8)], rr.at[n], g,
            r_send.at[n], r_recv.at[n],
        )
        exchange(*right_g)
        rr[n, g] = rs[n, p]

        if n == 0:
            arrive(*left_z)
            parts = [
                [
                    jnp.concatenate(
                        [
                            short_r[zh_ * 8 + zl_].astype(f32),
                            lent_rows(zr[n, 1, zh_ * 8 + zl_].astype(f32), roll_lanes),
                        ],
                        axis=0,
                    )
                    for zl_ in range(8)
                ]
                for zh_ in range(2)
            ]
        else:
            @pl.when(from_own)
            def _():
                all_bytes(zr.at[1, 0], 15, z_recv.at[1, 0]).wait()

            @pl.when(jnp.logical_not(from_own))
            def _():
                all_bytes(zr.at[1, 0], 16, z_recv.at[1, 0]).wait()

            parts = [
                [zr[n, 0, x_ * 4 + zh_ * 2 + zlo].astype(f32) for x_ in range(4) for zlo in range(2)]
                for zh_ in range(2)
            ]
        for zh_ in range(2):
            for i, values in regroup(parts[zh_], roll_lanes):
                wide[pl.ds(zh_ * 24 + i, 8, stride=48), :] = values
        for c in range(8):
            ls[n, c] = wide[c * 48 : c * 48 + 48, :].astype(bf16)
        left_g = (
            g_peer, P_STEPS, lambda other: ls.at[n, lax.rem(other, 8)], ll.at[n], g,
            l_send.at[n], l_recv.at[n],
        )
        exchange(*left_g)
        ll[n, g] = ls[n, p]
        arrive(*right_g)
        unpacked = unpack_rows(rr[n], roll_lanes)
        rights = assemble(lambda x_, p_: unpacked[x_ * 8 + p_])
        arrive(*left_g)
        if n == 0:
            lefts = jnp.concatenate(
                [
                    jnp.concatenate([ll[n, x * 8 + y_ * 2 + core_] for y_ in range(4)], axis=1)
                    for core_ in range(2)
                ],
                axis=0,
            )
            total = product_out(lefts, rights, columns[...])
        else:
            total = product_in(lambda p_: ll[n, x * 8 + p_], rights, rows[...], roll_lanes)

        for other in range(8):
            there, far = other % 2, other // 2
            c1s[n, other] = total[there * 48 : there * 48 + 48, far * 128 : far * 128 + 128].astype(bf16)
        c1 = (
            g_peer, P_STEPS, lambda other: c1s.at[n, lax.rem(other, 8)], c1r.at[n], g,
            c1_send.at[n], c1_recv.at[n],
        )
        exchange(*c1)
        c1r[n, g] = c1s[n, p]
        arrive(*c1)
        parts = swap_lanes([c1r[n, x * 8 + other].astype(f32) for other in range(8)], 16, roll_lanes)
        for other in range(16):
            start = (other // 8) * 24
            c2s[n, other] = parts[other % 8][start : start + 24].astype(bf16)
        c2 = (
            z_peer, Z_STEPS, lambda other: c2s.at[n, other], c2r.at[n], z,
            c2_send.at[n], c2_recv.at[n],
        )
        exchange(*c2)
        c2r[n, z] = c2s[n, z]
        later[2 * n].wait()
        arrive(*c2)
        combined = unfold([c2r[n, other].astype(f32) for other in range(16)], roll_lanes)
        return finish(state, combined, gate, o_ref[...])

    first_loads[0].wait()
    for k in range(12):
        for ih in range(3):
            block[pl.ds(ih * 16 + k, 8, stride=48), :] = x_ref[k, ih * 8 : ih * 8 + 8].astype(f32)
    state = block[...].astype(bf16)
    state = triangle(0, state, w1_ref, o1_ref)
    state = triangle(1, state, w2_ref, o2_ref)
    block[...] = state.astype(f32)
    state = jnp.concatenate(
        [block[pl.ds(ih * 16 + k, 8, stride=48), :] for k in range(12) for ih in range(3)], axis=0
    )
    normed = layer_norm(state).astype(bf16)
    later[3].wait()
    later[4].wait()
    hidden = nn(normed, t1_ref[...])
    mixed = (jax.nn.silu(hidden[:, :512]) * hidden[:, 512:]).astype(bf16)
    result = (state + nn(mixed, t2_ref[...])).astype(bf16)
    for k in range(12):
        out_ref[k] = result[k * 24 : k * 24 + 24]
    for target, count, send in sent:
        all_bytes(target, count, send).wait()

    @pl.when(from_own)
    def _():
        all_bytes(zs.at[1, 0], 15, z_send.at[1, 0]).wait()

    @pl.when(jnp.logical_not(from_own))
    def _():
        all_bytes(zs.at[1, 0], 16, z_send.at[1, 0]).wait()


def body(pair_state, *weights):
    dma = pltpu.SemaphoreType.DMA
    out = pl.pallas_call(
        kernel,
        out_shape=jax.ShapeDtypeStruct((12, 24, 128), bf16),
        in_specs=[pl.BlockSpec(memory_space=pltpu.HBM)] * 7,
        out_specs=pl.BlockSpec(memory_space=pltpu.VMEM),
        scratch_shapes=[pltpu.VMEM((12, 24, 128), bf16)]
        + [pltpu.VMEM(weight.shape, bf16) for weight in weights]
        + [
            pltpu.VMEM((384, 128), f32),
            pltpu.VMEM((384, 512), bf16),
            pltpu.VMEM((96, 128), bf16),
            pltpu.VMEM((2, 2, 16, 24, 128), bf16),
            pltpu.VMEM((2, 2, 16, 24, 128), bf16),
            pltpu.VMEM((16, 16, 128), bf16),
            pltpu.VMEM((16, 16, 128), bf16),
            pltpu.VMEM((384, 128), f32),
            pltpu.VMEM((320, 128), f32),
            pltpu.VMEM((2, 8, 40, 128), bf16),
            pltpu.VMEM((2, 32, 40, 128), bf16),
            pltpu.VMEM((2, 8, 48, 128), bf16),
            pltpu.VMEM((2, 32, 48, 128), bf16),
            pltpu.VMEM((2, 8, 48, 128), bf16),
            pltpu.VMEM((2, 32, 48, 128), bf16),
            pltpu.VMEM((2, 16, 24, 128), bf16),
            pltpu.VMEM((2, 16, 24, 128), bf16),
            dma((7,)),
            dma((2, 2)), dma((2, 2)),
            dma((2,)), dma((2,)),
            dma((2,)), dma((2,)),
            dma((2,)), dma((2,)),
            dma((2,)), dma((2,)),
        ],
        compiler_params=pltpu.CompilerParams(
            collective_id=0, has_side_effects=True, vmem_limit_bytes=60 * 2**20
        ),
    )(pair_state.transpose(1, 0, 2), *weights)
    return out.transpose(1, 0, 2)


def solution(mesh):
    placed = (P("row", "col", None), P(), P(), P(), P(), P(), P())
    return jax.shard_map(
        body, mesh=mesh, in_specs=placed, out_specs=P("row", "col", None), check_vma=False
    )
```

```python
import jax
import jax.numpy as jnp
from jax import lax
from jax.experimental import pallas as pl
from jax.experimental.pallas import tpu as pltpu
from jax.sharding import PartitionSpec as P

MESH = pl.DeviceIdType.MESH
norm_eps = 1e-05
f32 = jnp.float32
bf16 = jnp.bfloat16

Z_STEPS = (8, 7, 9, 6, 10, 5, 11, 4, 12, 3, 13, 2, 14, 1, 15)


def far_first(steps):
    def hops(step):
        return min(step[0], 4 - step[0]) + min(step[1], 4 - step[1]) + step[2]

    return tuple(sorted(steps, key=lambda step: (-hops(step), -min(step[1], 4 - step[1]), step[0], step[1])))


P_STEPS = far_first((0, dy, dc) for dy in range(4) for dc in range(2) if (dy, dc) != (0, 0))
G_STEPS = far_first(
    (dx, dy, dc) for dx in range(4) for dy in range(4) for dc in range(2) if (dx, dy, dc) != (0, 0, 0)
)


def roll_lanes(values, shift):
    return pltpu.roll(values, shift, 1)


def swap_lanes(parts, width, roll, bits=(1, 2, 4)):
    lane = lax.broadcasted_iota(jnp.int32, parts[0].shape, 1)
    parts = list(parts)
    for bit in bits:
        low = (lane & (bit * width)) == 0
        for a in range(len(parts)):
            if a & bit == 0:
                first, second = parts[a], parts[a | bit]
                parts[a] = jnp.where(low, first, roll(second, bit * width))
                parts[a | bit] = jnp.where(low, roll(first, 128 - bit * width), second)
    return parts


def layer_norm(values):
    centred = values - jnp.mean(values, axis=-1, keepdims=True)
    spread = jnp.mean(centred * centred, axis=-1, keepdims=True)
    return centred * lax.rsqrt(spread + norm_eps)


def nt(a, b):
    return lax.dot_general(a, b, (((1,), (1,)), ((), ())), preferred_element_type=f32)


def nn(a, b):
    return jnp.dot(a, b, preferred_element_type=f32)


def ones_where(shape, row_of):
    row = lax.broadcasted_iota(jnp.int32, shape, 0)
    column = lax.broadcasted_iota(jnp.int32, shape, 1)
    return jnp.where((row == row_of(column)) & ((column & 15) < 12), 1.0, 0.0).astype(bf16)


def column_places():
    return ones_where(
        (384, 512),
        lambda n: ((n >> 5) & 3) * 96 + (n >> 8) * 48 + ((n >> 4) & 1) * 24 + ((n >> 7) & 1) * 12 + (n & 15),
    )


def row_places():
    return ones_where((96, 128), lambda n: (n >> 6) * 48 + ((n >> 4) & 1) * 24 + ((n >> 5) & 1) * 12 + (n & 15))


def order_rows(normed):
    return jnp.concatenate(
        [normed[(il * 3 + ih) * 16 : (il * 3 + ih + 1) * 16] for ih in range(3) for il in range(8)], axis=0
    )


def edge(ordered, w_t):
    projected = nt(w_t, ordered)
    return jax.nn.sigmoid(projected[0:128]) * projected[128:256]


def z_parcel(values, z, groups=3):
    return jnp.concatenate([values[z * 8 : z * 8 + 8, ih * 128 : ih * 128 + 128] for ih in range(groups)], axis=0)


def lend_lanes(right, left, roll):
    spare = (lax.broadcasted_iota(jnp.int32, (128, 128), 1) & 15) >= 12
    return jnp.concatenate(
        [
            jnp.where(spare, roll(left[:, 256:384], 12 - 4 * ih), right[:, ih * 128 : ih * 128 + 128])
            for ih in range(3)
        ],
        axis=1,
    )


def lent_rows(right, roll):
    thirds = [roll(right[ih * 8 : ih * 8 + 8], 116 + 4 * ih) for ih in range(3)]
    inside = lax.broadcasted_iota(jnp.int32, (8, 128), 1) & 15
    last = jnp.where(inside < 12, thirds[2], 0.0)
    return jnp.where(inside < 4, thirds[0], jnp.where(inside < 8, thirds[1], last))


def regroup(parts, roll):
    for ih in range(3):
        swapped = swap_lanes([part[ih * 8 : ih * 8 + 8] for part in parts], 16, roll)
        for il in range(8):
            yield ih * 8 + il, swapped[il]


def pack_rows(rows, roll):
    spare = (lax.broadcasted_iota(jnp.int32, rows[0].shape, 1) & 15) >= 12
    packed = list(rows[:40])
    for third in range(3):
        for a in range(8):
            b = third * 8 + a
            packed[b] = jnp.where(spare, roll(rows[40 + a], 12 - 4 * third), packed[b])
    return packed


def unpack_rows(packed, roll, clean=False):
    count = packed.shape[0]
    packed = packed.astype(f32)
    thirds = [
        roll(packed[:, third * 8 : third * 8 + 8].reshape(count * 8, 128), 116 + 4 * third) for third in range(3)
    ]
    inside = lax.broadcasted_iota(jnp.int32, thirds[0].shape, 1) & 15
    last = jnp.where(inside < 4, thirds[0], jnp.where(inside < 8, thirds[1], thirds[2]))
    whole = jnp.concatenate([packed, last.reshape(count, 8, 128)], axis=1)
    if clean:
        whole = jnp.where((lax.broadcasted_iota(jnp.int32, whole.shape, 2) & 15) < 12, whole, 0.0)
    return whole.astype(bf16)


def assemble(parts):
    return jnp.concatenate(
        [
            jnp.concatenate([parts(x, y * 2 + core) for y in range(4)], axis=1)
            for x in range(4)
            for core in range(2)
        ],
        axis=0,
    )


def product_out(left, right, places):
    return nn(nt(left, right).astype(bf16), places)


def product_in(left, right, places, roll):
    cores = [swap_lanes([left(y * 2 + core).astype(f32) for y in range(4)], 32, roll, (1, 2)) for core in range(2)]
    rows = jnp.concatenate([cores[core][x] for x in range(4) for core in range(2)], axis=0)
    return nn(nt(places, rows.astype(bf16)).astype(bf16), right)


def unfold(parts, roll):
    columns = [[] for _ in range(8)]
    for ih in range(3):
        turned = jnp.concatenate([part[ih * 8 : ih * 8 + 8] for part in parts], axis=0).T
        for p in range(8):
            columns[p].append(turned[p * 16 : p * 16 + 16])
    return jnp.concatenate(swap_lanes([jnp.concatenate(part, axis=0) for part in columns], 1, roll), axis=0)


def finish(state, combined, gate, weight):
    update = nn(layer_norm(combined).astype(bf16), weight)
    return (state.astype(f32) + gate * update).astype(bf16)


def kernel(
    x_hbm, w1_hbm, o1_hbm, w2_hbm, o2_hbm, t1_hbm, t2_hbm, out_ref,
    x_ref, w1_ref, o1_ref, w2_ref, o2_ref, t1_ref, t2_ref,
    block, columns, rows, zs, zr, short_s, short_r, wide, narrow, rs, rr, ls, ll, c1s, c1r, c2s, c2r,
    load_sem, z_send, z_recv, r_send, r_recv, l_send, l_recv, c1_send, c1_recv, c2_send, c2_recv,
):
    row, col = lax.axis_index("row"), lax.axis_index("col")
    x, zh, core = row // 4, (row // 2) % 2, row % 2
    zl, y = col // 4, col % 4
    z, p = zh * 8 + zl, y * 2 + core
    g = x * 8 + p
    far_x = zl // 2
    from_own = far_x == x

    def z_place(at_x, at_z):
        return ((at_x * 2 + at_z // 8) * 2 + core, lax.rem(at_z, 8) * 4 + y)

    def z_peer(step):
        other = lax.rem(z + step, 16)
        return other, z_place(x, other)

    def g_peer(step):
        dx, dy, dc = step
        other_x, other_y, other_core = lax.rem(x + dx, 4), lax.rem(y + dy, 4), lax.rem(core + dc, 2)
        return (
            other_x * 8 + other_y * 2 + other_core,
            ((other_x * 2 + zh) * 2 + other_core, zl * 4 + other_y),
        )

    def load(i, source, target):
        copy = pltpu.make_async_copy(source, target, load_sem.at[i])
        copy.start()
        return copy

    first_loads = [load(0, x_hbm, x_ref), load(1, w1_hbm, w1_ref)]

    barrier = pltpu.get_barrier_semaphore()
    for step in Z_STEPS:
        pl.semaphore_signal(barrier, inc=1, device_id=z_peer(step)[1], device_id_type=MESH)
    for dx in (2, 1, 3):
        for source in range(4):
            at_z = (source // 2) * 8 + x * 2 + source % 2
            pl.semaphore_signal(
                barrier, inc=1, device_id=z_place(lax.rem(x + dx, 4), at_z), device_id_type=MESH
            )
    for step in G_STEPS:
        pl.semaphore_signal(barrier, inc=1, device_id=g_peer(step)[1], device_id_type=MESH)
    greeted = len(Z_STEPS) + len(G_STEPS) + jnp.where(from_own, 0, 16)

    columns[...] = column_places()
    rows[...] = row_places()
    block[...] = jnp.zeros_like(block)

    sent = []

    def exchange(peer, steps, source, target, me, send, recv):
        for step in steps:
            other, place = peer(step)
            pltpu.make_async_remote_copy(
                src_ref=source(other), dst_ref=target.at[me], send_sem=send, recv_sem=recv,
                device_id=place, device_id_type=MESH,
            ).start()
        sent.append((target, len(steps), send))

    def all_bytes(target, count, sem):
        blocks = target.at[pl.ds(0, count)]
        return pltpu.make_async_copy(blocks, blocks, sem)

    def arrive(peer, steps, source, target, me, send, recv):
        all_bytes(target, len(steps), recv).wait()

    def far_copy(step):
        other = lax.rem(z + step, 16)
        pltpu.make_async_remote_copy(
            src_ref=zs.at[1, 0, other], dst_ref=zr.at[1, 0, x * 4 + zh * 2 + lax.rem(zl, 2)],
            send_sem=z_send.at[1, 0], recv_sem=z_recv.at[1, 0],
            device_id=z_place(far_x, other), device_id_type=MESH,
        ).start()

    later = []

    def triangle(n, state, w_ref, o_ref):
        normed = layer_norm(state.astype(f32)).astype(bf16)
        ordered = order_rows(normed)
        (first_loads[1] if n == 0 else later[1]).wait()

        def edges(s):
            return edge(ordered, w_ref[:, s * 256 : s * 256 + 256].T)

        right = edges(1)
        if n == 0:
            left = edges(0)
            right = lend_lanes(right, left, roll_lanes)
        for other in range(16):
            zs[n, 1, other] = z_parcel(right, other).astype(bf16)
        right_z = (
            z_peer, Z_STEPS, lambda other: zs.at[n, 1, other], zr.at[n, 1], z, z_send.at[n, 1], z_recv.at[n, 1]
        )
        if n == 0:
            pl.semaphore_wait(barrier, greeted)
        exchange(*right_z)
        zr[n, 1, z] = zs[n, 1, z]
        slot = x * 4 + zh * 2 + lax.rem(zl, 2)
        if n == 0:
            for other in range(16):
                short_s[other] = z_parcel(left, other, 2).astype(bf16)
            left_z = (
                z_peer, Z_STEPS, lambda other: short_s.at[other], short_r, z, z_send.at[n, 0], z_recv.at[n, 0]
            )
            exchange(*left_z)
            short_r[z] = short_s[z]
            for i, (source, target) in enumerate(
                ((o1_hbm, o1_ref), (w2_hbm, w2_ref), (o2_hbm, o2_ref), (t1_hbm, t1_ref), (t2_hbm, t2_ref))
            ):
                later.append(load(2 + i, source, target))
        else:
            left = edges(0)
            for other in range(16):
                zs[n, 0, other] = z_parcel(left, other).astype(bf16)
            for step in Z_STEPS:
                far_copy(step)

            @pl.when(jnp.logical_not(from_own))
            def _():
                far_copy(0)

            @pl.when(from_own)
            def _():
                zr[1, 0, slot] = zs[1, 0, z]

        gate = jax.nn.sigmoid(nn(normed, w_ref[:, 512:640]))

        arrive(*right_z)
        values = [
            value
            for zh_ in range(2)
            for _, value in regroup([zr[n, 1, zh_ * 8 + zl_].astype(f32) for zl_ in range(8)], roll_lanes)
        ]
        for i, value in enumerate(pack_rows(values, roll_lanes)):
            narrow[pl.ds(i, 8, stride=40), :] = value
        for c in range(8):
            rs[n, c] = narrow[c * 40 : c * 40 + 40, :].astype(bf16)
        right_g = (
            g_peer, G_STEPS, lambda other: rs.at[n, lax.rem(other, 8)], rr.at[n], g,
            r_send.at[n], r_recv.at[n],
        )
        exchange(*right_g)
        rr[n, g] = rs[n, p]

        if n == 0:
            arrive(*left_z)
            parts = [
                [
                    jnp.concatenate(
                        [
                            short_r[zh_ * 8 + zl_].astype(f32),
                            lent_rows(zr[n, 1, zh_ * 8 + zl_].astype(f32), roll_lanes),
                        ],
                        axis=0,
                    )
                    for zl_ in range(8)
                ]
                for zh_ in range(2)
            ]
        else:
            @pl.when(from_own)
            def _():
                all_bytes(zr.at[1, 0], 15, z_recv.at[1, 0]).wait()

            @pl.when(jnp.logical_not(from_own))
            def _():
                all_bytes(zr.at[1, 0], 16, z_recv.at[1, 0]).wait()

            parts = [
                [zr[n, 0, x_ * 4 + zh_ * 2 + zlo].astype(f32) for x_ in range(4) for zlo in range(2)]
                for zh_ in range(2)
            ]
        values = [value for zh_ in range(2) for _, value in regroup(parts[zh_], roll_lanes)]
        for i, value in enumerate(pack_rows(values, roll_lanes)):
            wide[pl.ds(i, 8, stride=40), :] = value
        for c in range(8):
            ls[n, c] = wide[c * 40 : c * 40 + 40, :].astype(bf16)
        left_g = (
            g_peer, P_STEPS, lambda other: ls.at[n, lax.rem(other, 8)], ll.at[n], g,
            l_send.at[n], l_recv.at[n],
        )
        exchange(*left_g)
        ll[n, g] = ls[n, p]
        arrive(*right_g)
        unpacked = unpack_rows(rr[n], roll_lanes)
        rights = assemble(lambda x_, p_: unpacked[x_ * 8 + p_])
        arrive(*left_g)
        own = unpack_rows(ll[n, pl.ds(x * 8, 8)], roll_lanes, clean=n == 0)
        if n == 0:
            lefts = jnp.concatenate(
                [
                    jnp.concatenate([own[y_ * 2 + core_] for y_ in range(4)], axis=1)
                    for core_ in range(2)
                ],
                axis=0,
            )
            total = product_out(lefts, rights, columns[...])
        else:
            total = product_in(lambda p_: own[p_], rights, rows[...], roll_lanes)

        for other in range(8):
            there, far = other % 2, other // 2
            c1s[n, other] = total[there * 48 : there * 48 + 48, far * 128 : far * 128 + 128].astype(bf16)
        c1 = (
            g_peer, P_STEPS, lambda other: c1s.at[n, lax.rem(other, 8)], c1r.at[n], g,
            c1_send.at[n], c1_recv.at[n],
        )
        exchange(*c1)
        c1r[n, g] = c1s[n, p]
        arrive(*c1)
        parts = swap_lanes([c1r[n, x * 8 + other].astype(f32) for other in range(8)], 16, roll_lanes)
        for other in range(16):
            start = (other // 8) * 24
            c2s[n, other] = parts[other % 8][start : start + 24].astype(bf16)
        c2 = (
            z_peer, Z_STEPS, lambda other: c2s.at[n, other], c2r.at[n], z,
            c2_send.at[n], c2_recv.at[n],
        )
        exchange(*c2)
        c2r[n, z] = c2s[n, z]
        later[2 * n].wait()
        arrive(*c2)
        combined = unfold([c2r[n, other].astype(f32) for other in range(16)], roll_lanes)
        return finish(state, combined, gate, o_ref[...])

    first_loads[0].wait()
    for k in range(12):
        for ih in range(3):
            block[pl.ds(ih * 16 + k, 8, stride=48), :] = x_ref[k, ih * 8 : ih * 8 + 8].astype(f32)
    state = block[...].astype(bf16)
    state = triangle(0, state, w1_ref, o1_ref)
    state = triangle(1, state, w2_ref, o2_ref)
    normed = layer_norm(state.astype(f32)).astype(bf16)
    later[3].wait()
    later[4].wait()
    hidden = nn(normed, t1_ref[...])
    mixed = (jax.nn.silu(hidden[:, :512]) * hidden[:, 512:]).astype(bf16)
    block[...] = state.astype(f32) + nn(mixed, t2_ref[...])
    for k in range(12):
        out_ref[k] = jnp.concatenate(
            [block[pl.ds(ih * 16 + k, 8, stride=48), :] for ih in range(3)], axis=0
        ).astype(bf16)
    for target, count, send in sent:
        all_bytes(target, count, send).wait()

    @pl.when(from_own)
    def _():
        all_bytes(zs.at[1, 0], 15, z_send.at[1, 0]).wait()

    @pl.when(jnp.logical_not(from_own))
    def _():
        all_bytes(zs.at[1, 0], 16, z_send.at[1, 0]).wait()


def body(pair_state, *weights):
    dma = pltpu.SemaphoreType.DMA
    out = pl.pallas_call(
        kernel,
        out_shape=jax.ShapeDtypeStruct((12, 24, 128), bf16),
        in_specs=[pl.BlockSpec(memory_space=pltpu.HBM)] * 7,
        out_specs=pl.BlockSpec(memory_space=pltpu.VMEM),
        scratch_shapes=[pltpu.VMEM((12, 24, 128), bf16)]
        + [pltpu.VMEM(weight.shape, bf16) for weight in weights]
        + [
            pltpu.VMEM((384, 128), f32),
            pltpu.VMEM((384, 512), bf16),
            pltpu.VMEM((96, 128), bf16),
            pltpu.VMEM((2, 2, 16, 24, 128), bf16),
            pltpu.VMEM((2, 2, 16, 24, 128), bf16),
            pltpu.VMEM((16, 16, 128), bf16),
            pltpu.VMEM((16, 16, 128), bf16),
            pltpu.VMEM((320, 128), f32),
            pltpu.VMEM((320, 128), f32),
            pltpu.VMEM((2, 8, 40, 128), bf16),
            pltpu.VMEM((2, 32, 40, 128), bf16),
            pltpu.VMEM((2, 8, 40, 128), bf16),
            pltpu.VMEM((2, 32, 40, 128), bf16),
            pltpu.VMEM((2, 8, 48, 128), bf16),
            pltpu.VMEM((2, 32, 48, 128), bf16),
            pltpu.VMEM((2, 16, 24, 128), bf16),
            pltpu.VMEM((2, 16, 24, 128), bf16),
            dma((7,)),
            dma((2, 2)), dma((2, 2)),
            dma((2,)), dma((2,)),
            dma((2,)), dma((2,)),
            dma((2,)), dma((2,)),
            dma((2,)), dma((2,)),
        ],
        compiler_params=pltpu.CompilerParams(
            collective_id=0, has_side_effects=True, vmem_limit_bytes=60 * 2**20
        ),
    )(pair_state.transpose(1, 0, 2), *weights)
    return out.transpose(1, 0, 2)


def solution(mesh):
    placed = (P("row", "col", None), P(), P(), P(), P(), P(), P())
    return jax.shard_map(
        body, mesh=mesh, in_specs=placed, out_specs=P("row", "col", None), check_vma=False
    )
```

```python
import jax
import jax.numpy as jnp
from jax import lax
from jax.experimental import pallas as pl
from jax.experimental.pallas import tpu as pltpu
from jax.sharding import PartitionSpec as P

MESH = pl.DeviceIdType.MESH
norm_eps = 1e-05
f32 = jnp.float32
bf16 = jnp.bfloat16

Z_STEPS = (8, 7, 9, 6, 10, 5, 11, 4, 12, 3, 13, 2, 14, 1, 15)


def far_first(steps):
    def hops(step):
        return min(step[0], 4 - step[0]) + min(step[1], 4 - step[1]) + step[2]

    return tuple(sorted(steps, key=lambda step: (-hops(step), -min(step[1], 4 - step[1]), step[0], step[1])))


P_STEPS = far_first((0, dy, dc) for dy in range(4) for dc in range(2) if (dy, dc) != (0, 0))
G_STEPS = far_first(
    (dx, dy, dc) for dx in range(4) for dy in range(4) for dc in range(2) if (dx, dy, dc) != (0, 0, 0)
)


def roll_lanes(values, shift):
    return pltpu.roll(values, shift, 1)


def swap_lanes(parts, width, roll, bits=(1, 2, 4)):
    lane = lax.broadcasted_iota(jnp.int32, parts[0].shape, 1)
    parts = list(parts)
    for bit in bits:
        low = (lane & (bit * width)) == 0
        for a in range(len(parts)):
            if a & bit == 0:
                first, second = parts[a], parts[a | bit]
                parts[a] = jnp.where(low, first, roll(second, bit * width))
                parts[a | bit] = jnp.where(low, roll(first, 128 - bit * width), second)
    return parts


def layer_norm(values):
    centred = values - jnp.mean(values, axis=-1, keepdims=True)
    spread = jnp.mean(centred * centred, axis=-1, keepdims=True)
    return centred * lax.rsqrt(spread + norm_eps)


def nt(a, b):
    return lax.dot_general(a, b, (((1,), (1,)), ((), ())), preferred_element_type=f32)


def nn(a, b):
    return jnp.dot(a, b, preferred_element_type=f32)


def ones_where(shape, row_of):
    row = lax.broadcasted_iota(jnp.int32, shape, 0)
    column = lax.broadcasted_iota(jnp.int32, shape, 1)
    return jnp.where((row == row_of(column)) & ((column & 15) < 12), 1.0, 0.0).astype(bf16)


def column_places():
    return ones_where(
        (384, 512),
        lambda n: ((n >> 5) & 3) * 96 + (n >> 8) * 48 + ((n >> 4) & 1) * 24 + ((n >> 7) & 1) * 12 + (n & 15),
    )


def row_places():
    return ones_where((96, 128), lambda n: (n >> 6) * 48 + ((n >> 4) & 1) * 24 + ((n >> 5) & 1) * 12 + (n & 15))


def order_rows(normed):
    return jnp.concatenate(
        [normed[(il * 3 + ih) * 16 : (il * 3 + ih + 1) * 16] for ih in range(3) for il in range(8)], axis=0
    )


def edge(ordered, w_t):
    projected = nt(w_t, ordered)
    return jax.nn.sigmoid(projected[0:128]) * projected[128:256]


def z_parcel(values, z, groups=3):
    return jnp.concatenate([values[z * 8 : z * 8 + 8, ih * 128 : ih * 128 + 128] for ih in range(groups)], axis=0)


def lend_lanes(right, left, roll):
    spare = (lax.broadcasted_iota(jnp.int32, (128, 128), 1) & 15) >= 12
    return jnp.concatenate(
        [
            jnp.where(spare, roll(left[:, 256:384], 12 - 4 * ih), right[:, ih * 128 : ih * 128 + 128])
            for ih in range(3)
        ],
        axis=1,
    )


def lent_rows(right, roll):
    thirds = [roll(right[ih * 8 : ih * 8 + 8], 116 + 4 * ih) for ih in range(3)]
    inside = lax.broadcasted_iota(jnp.int32, (8, 128), 1) & 15
    last = jnp.where(inside < 12, thirds[2], 0.0)
    return jnp.where(inside < 4, thirds[0], jnp.where(inside < 8, thirds[1], last))


def regroup(parts, roll):
    for ih in range(3):
        swapped = swap_lanes([part[ih * 8 : ih * 8 + 8] for part in parts], 16, roll)
        for il in range(8):
            yield ih * 8 + il, swapped[il]


def pack_rows(rows, roll):
    spare = (lax.broadcasted_iota(jnp.int32, rows[0].shape, 1) & 15) >= 12
    packed = list(rows[:40])
    for third in range(3):
        for a in range(8):
            b = third * 8 + a
            packed[b] = jnp.where(spare, roll(rows[40 + a], 12 - 4 * third), packed[b])
    return packed


def unpack_rows(packed, roll):
    count = packed.shape[0]
    packed = packed.astype(f32)
    thirds = [
        roll(packed[:, third * 8 : third * 8 + 8].reshape(count * 8, 128), 116 + 4 * third) for third in range(3)
    ]
    inside = lax.broadcasted_iota(jnp.int32, thirds[0].shape, 1) & 15
    last = jnp.where(inside < 4, thirds[0], jnp.where(inside < 8, thirds[1], thirds[2]))
    return jnp.concatenate([packed, last.reshape(count, 8, 128)], axis=1).astype(bf16)


def assemble(parts):
    return jnp.concatenate(
        [
            jnp.concatenate([parts(x, y * 2 + core) for y in range(4)], axis=1)
            for x in range(4)
            for core in range(2)
        ],
        axis=0,
    )


def product_out(left, right, places):
    return nn(nt(left, right).astype(bf16), places)


def product_in(left, right, places, roll):
    cores = [swap_lanes([left(y * 2 + core).astype(f32) for y in range(4)], 32, roll, (1, 2)) for core in range(2)]
    rows = jnp.concatenate([cores[core][x] for x in range(4) for core in range(2)], axis=0)
    return nn(nt(places, rows.astype(bf16)).astype(bf16), right)


def unfold(parts, roll):
    columns = [[] for _ in range(8)]
    for ih in range(3):
        turned = jnp.concatenate([part[ih * 8 : ih * 8 + 8] for part in parts], axis=0).T
        for p in range(8):
            columns[p].append(turned[p * 16 : p * 16 + 16])
    return jnp.concatenate(swap_lanes([jnp.concatenate(part, axis=0) for part in columns], 1, roll), axis=0)


def finish(state, combined, gate, weight):
    update = nn(layer_norm(combined).astype(bf16), weight)
    return (state.astype(f32) + gate * update).astype(bf16)


def kernel(
    x_hbm, w1_hbm, o1_hbm, w2_hbm, o2_hbm, t1_hbm, t2_hbm, out_ref,
    x_ref, w1_ref, o1_ref, w2_ref, o2_ref, t1_ref, t2_ref,
    block, columns, rows, zs, zr, short_s, short_r, wide, narrow, rs, rr, ls, ll, c1s, c1r, c2s, c2r,
    load_sem, z_send, z_recv, r_send, r_recv, l_send, l_recv, c1_send, c1_recv, c2_send, c2_recv,
):
    row, col = lax.axis_index("row"), lax.axis_index("col")
    x, zh, core = row // 4, (row // 2) % 2, row % 2
    zl, y = col // 4, col % 4
    z, p = zh * 8 + zl, y * 2 + core
    g = x * 8 + p
    far_x = zl // 2
    from_own = far_x == x

    def z_place(at_x, at_z):
        return ((at_x * 2 + at_z // 8) * 2 + core, lax.rem(at_z, 8) * 4 + y)

    def z_peer(step):
        other = lax.rem(z + step, 16)
        return other, z_place(x, other)

    def g_peer(step):
        dx, dy, dc = step
        other_x, other_y, other_core = lax.rem(x + dx, 4), lax.rem(y + dy, 4), lax.rem(core + dc, 2)
        return (
            other_x * 8 + other_y * 2 + other_core,
            ((other_x * 2 + zh) * 2 + other_core, zl * 4 + other_y),
        )

    def load(i, source, target):
        copy = pltpu.make_async_copy(source, target, load_sem.at[i])
        copy.start()
        return copy

    first_loads = [load(0, x_hbm, x_ref), load(1, w1_hbm, w1_ref)]

    barrier = pltpu.get_barrier_semaphore()
    for step in Z_STEPS:
        pl.semaphore_signal(barrier, inc=1, device_id=z_peer(step)[1], device_id_type=MESH)
    for dx in (2, 1, 3):
        for source in range(4):
            at_z = (source // 2) * 8 + x * 2 + source % 2
            pl.semaphore_signal(
                barrier, inc=1, device_id=z_place(lax.rem(x + dx, 4), at_z), device_id_type=MESH
            )
    for step in G_STEPS:
        pl.semaphore_signal(barrier, inc=1, device_id=g_peer(step)[1], device_id_type=MESH)
    greeted = len(Z_STEPS) + len(G_STEPS) + jnp.where(from_own, 0, 16)

    columns[...] = column_places()
    rows[...] = row_places()
    block[...] = jnp.zeros_like(block)

    sent = []

    def exchange(peer, steps, source, target, me, send, recv, part=None):
        for step in steps if part is None else part:
            other, place = peer(step)
            pltpu.make_async_remote_copy(
                src_ref=source(other), dst_ref=target.at[me], send_sem=send, recv_sem=recv,
                device_id=place, device_id_type=MESH,
            ).start()
        if part is None or part[-1] == steps[-1]:
            sent.append((target, len(steps), send))

    def all_bytes(target, count, sem):
        blocks = target.at[pl.ds(0, count)]
        return pltpu.make_async_copy(blocks, blocks, sem)

    def arrive(peer, steps, source, target, me, send, recv):
        all_bytes(target, len(steps), recv).wait()

    def far_copy(step):
        other = lax.rem(z + step, 16)
        pltpu.make_async_remote_copy(
            src_ref=zs.at[1, 0, other], dst_ref=zr.at[1, 0, x * 4 + zh * 2 + lax.rem(zl, 2)],
            send_sem=z_send.at[1, 0], recv_sem=z_recv.at[1, 0],
            device_id=z_place(far_x, other), device_id_type=MESH,
        ).start()

    later = []

    def triangle(n, state, w_ref, o_ref):
        normed = layer_norm(state.astype(f32)).astype(bf16)
        ordered = order_rows(normed)
        (first_loads[1] if n == 0 else later[1]).wait()

        def edges(s):
            return edge(ordered, w_ref[:, s * 256 : s * 256 + 256].T)

        right = edges(1)
        if n == 0:
            left = edges(0)
            right = lend_lanes(right, left, roll_lanes)
        for other in range(16):
            zs[n, 1, other] = z_parcel(right, other).astype(bf16)
        right_z = (
            z_peer, Z_STEPS, lambda other: zs.at[n, 1, other], zr.at[n, 1], z, z_send.at[n, 1], z_recv.at[n, 1]
        )
        if n == 0:
            pl.semaphore_wait(barrier, greeted)
        exchange(*right_z, part=Z_STEPS[:9] if n == 0 else None)
        zr[n, 1, z] = zs[n, 1, z]
        slot = x * 4 + zh * 2 + lax.rem(zl, 2)
        if n == 0:
            for other in range(16):
                short_s[other] = z_parcel(left, other, 2).astype(bf16)
            left_z = (
                z_peer, Z_STEPS, lambda other: short_s.at[other], short_r, z, z_send.at[n, 0], z_recv.at[n, 0]
            )
            exchange(*left_z, part=Z_STEPS[:9])
            exchange(*right_z, part=Z_STEPS[9:])
            exchange(*left_z, part=Z_STEPS[9:])
            short_r[z] = short_s[z]
            for i, (source, target) in enumerate(
                ((o1_hbm, o1_ref), (w2_hbm, w2_ref), (o2_hbm, o2_ref), (t1_hbm, t1_ref), (t2_hbm, t2_ref))
            ):
                later.append(load(2 + i, source, target))
        else:
            left = edges(0)
            for other in range(16):
                zs[n, 0, other] = z_parcel(left, other).astype(bf16)
            for step in Z_STEPS:
                far_copy(step)

            @pl.when(jnp.logical_not(from_own))
            def _():
                far_copy(0)

            @pl.when(from_own)
            def _():
                zr[1, 0, slot] = zs[1, 0, z]

        gate = jax.nn.sigmoid(nn(normed, w_ref[:, 512:640]))

        arrive(*right_z)
        values = [
            value
            for zh_ in range(2)
            for _, value in regroup([zr[n, 1, zh_ * 8 + zl_].astype(f32) for zl_ in range(8)], roll_lanes)
        ]
        for i, value in enumerate(pack_rows(values, roll_lanes)):
            narrow[pl.ds(i, 8, stride=40), :] = value
        for c in range(8):
            rs[n, c] = narrow[c * 40 : c * 40 + 40, :].astype(bf16)
        right_g = (
            g_peer, G_STEPS, lambda other: rs.at[n, lax.rem(other, 8)], rr.at[n], g,
            r_send.at[n], r_recv.at[n],
        )
        exchange(*right_g)
        rr[n, g] = rs[n, p]

        if n == 0:
            arrive(*left_z)
            parts = [
                [
                    jnp.concatenate(
                        [
                            short_r[zh_ * 8 + zl_].astype(f32),
                            lent_rows(zr[n, 1, zh_ * 8 + zl_].astype(f32), roll_lanes),
                        ],
                        axis=0,
                    )
                    for zl_ in range(8)
                ]
                for zh_ in range(2)
            ]
        else:
            @pl.when(from_own)
            def _():
                all_bytes(zr.at[1, 0], 15, z_recv.at[1, 0]).wait()

            @pl.when(jnp.logical_not(from_own))
            def _():
                all_bytes(zr.at[1, 0], 16, z_recv.at[1, 0]).wait()

            parts = [
                [zr[n, 0, x_ * 4 + zh_ * 2 + zlo].astype(f32) for x_ in range(4) for zlo in range(2)]
                for zh_ in range(2)
            ]
        for zh_ in range(2):
            for i, values in regroup(parts[zh_], roll_lanes):
                wide[pl.ds(zh_ * 24 + i, 8, stride=48), :] = values
        for c in range(8):
            ls[n, c] = wide[c * 48 : c * 48 + 48, :].astype(bf16)
        left_g = (
            g_peer, P_STEPS, lambda other: ls.at[n, lax.rem(other, 8)], ll.at[n], g,
            l_send.at[n], l_recv.at[n],
        )
        exchange(*left_g)
        ll[n, g] = ls[n, p]
        arrive(*right_g)
        unpacked = unpack_rows(rr[n], roll_lanes)
        rights = assemble(lambda x_, p_: unpacked[x_ * 8 + p_])
        arrive(*left_g)
        if n == 0:
            lefts = jnp.concatenate(
                [
                    jnp.concatenate([ll[n, x * 8 + y_ * 2 + core_] for y_ in range(4)], axis=1)
                    for core_ in range(2)
                ],
                axis=0,
            )
            total = product_out(lefts, rights, columns[...])
        else:
            total = product_in(lambda p_: ll[n, x * 8 + p_], rights, rows[...], roll_lanes)

        for other in range(8):
            there, far = other % 2, other // 2
            c1s[n, other] = total[there * 48 : there * 48 + 48, far * 128 : far * 128 + 128].astype(bf16)
        c1 = (
            g_peer, P_STEPS, lambda other: c1s.at[n, lax.rem(other, 8)], c1r.at[n], g,
            c1_send.at[n], c1_recv.at[n],
        )
        exchange(*c1)
        c1r[n, g] = c1s[n, p]
        arrive(*c1)
        parts = swap_lanes([c1r[n, x * 8 + other].astype(f32) for other in range(8)], 16, roll_lanes)
        for other in range(16):
            start = (other // 8) * 24
            c2s[n, other] = parts[other % 8][start : start + 24].astype(bf16)
        c2 = (
            z_peer, Z_STEPS, lambda other: c2s.at[n, other], c2r.at[n], z,
            c2_send.at[n], c2_recv.at[n],
        )
        exchange(*c2)
        c2r[n, z] = c2s[n, z]
        later[2 * n].wait()
        arrive(*c2)
        combined = unfold([c2r[n, other].astype(f32) for other in range(16)], roll_lanes)
        return finish(state, combined, gate, o_ref[...])

    first_loads[0].wait()
    for k in range(12):
        for ih in range(3):
            block[pl.ds(ih * 16 + k, 8, stride=48), :] = x_ref[k, ih * 8 : ih * 8 + 8].astype(f32)
    state = block[...].astype(bf16)
    state = triangle(0, state, w1_ref, o1_ref)
    state = triangle(1, state, w2_ref, o2_ref)
    normed = layer_norm(state.astype(f32)).astype(bf16)
    later[3].wait()
    later[4].wait()
    hidden = nn(normed, t1_ref[...])
    mixed = (jax.nn.silu(hidden[:, :512]) * hidden[:, 512:]).astype(bf16)
    block[...] = state.astype(f32) + nn(mixed, t2_ref[...])
    for k in range(12):
        out_ref[k] = jnp.concatenate(
            [block[pl.ds(ih * 16 + k, 8, stride=48), :] for ih in range(3)], axis=0
        ).astype(bf16)
    for target, count, send in sent:
        all_bytes(target, count, send).wait()

    @pl.when(from_own)
    def _():
        all_bytes(zs.at[1, 0], 15, z_send.at[1, 0]).wait()

    @pl.when(jnp.logical_not(from_own))
    def _():
        all_bytes(zs.at[1, 0], 16, z_send.at[1, 0]).wait()


def body(pair_state, *weights):
    dma = pltpu.SemaphoreType.DMA
    out = pl.pallas_call(
        kernel,
        out_shape=jax.ShapeDtypeStruct((12, 24, 128), bf16),
        in_specs=[pl.BlockSpec(memory_space=pltpu.HBM)] * 7,
        out_specs=pl.BlockSpec(memory_space=pltpu.VMEM),
        scratch_shapes=[pltpu.VMEM((12, 24, 128), bf16)]
        + [pltpu.VMEM(weight.shape, bf16) for weight in weights]
        + [
            pltpu.VMEM((384, 128), f32),
            pltpu.VMEM((384, 512), bf16),
            pltpu.VMEM((96, 128), bf16),
            pltpu.VMEM((2, 2, 16, 24, 128), bf16),
            pltpu.VMEM((2, 2, 16, 24, 128), bf16),
            pltpu.VMEM((16, 16, 128), bf16),
            pltpu.VMEM((16, 16, 128), bf16),
            pltpu.VMEM((384, 128), f32),
            pltpu.VMEM((320, 128), f32),
            pltpu.VMEM((2, 8, 40, 128), bf16),
            pltpu.VMEM((2, 32, 40, 128), bf16),
            pltpu.VMEM((2, 8, 48, 128), bf16),
            pltpu.VMEM((2, 32, 48, 128), bf16),
            pltpu.VMEM((2, 8, 48, 128), bf16),
            pltpu.VMEM((2, 32, 48, 128), bf16),
            pltpu.VMEM((2, 16, 24, 128), bf16),
            pltpu.VMEM((2, 16, 24, 128), bf16),
            dma((7,)),
            dma((2, 2)), dma((2, 2)),
            dma((2,)), dma((2,)),
            dma((2,)), dma((2,)),
            dma((2,)), dma((2,)),
            dma((2,)), dma((2,)),
        ],
        compiler_params=pltpu.CompilerParams(
            collective_id=0, has_side_effects=True, vmem_limit_bytes=60 * 2**20
        ),
    )(pair_state.transpose(1, 0, 2), *weights)
    return out.transpose(1, 0, 2)


def solution(mesh):
    placed = (P("row", "col", None), P(), P(), P(), P(), P(), P())
    return jax.shard_map(
        body, mesh=mesh, in_specs=placed, out_specs=P("row", "col", None), check_vma=False
    )
```
